32 devices in a mesh: row: 4 (over y, x), col: 8 (over z, core).
Axes of the slice: x: 2, y: 2, z: 4, core: 2. Of those that a mesh axis runs over, the one named last changes fastest.
Arguments:
- features: bfloat16 [4096, 512], P(('row', 'col')), may hold values from -6 to 6
- adj_tiles: bfloat16 [4, 64, 128, 128], P('row', 'col'), may hold values from -0.1875 to 0.1875
- tile_rows: int32 [4, 64], P('row', 'col'), may hold values from 0 to 7, as said below
- tile_cols: int32 [4, 64], P('row', 'col'), may hold values from 0 to 3
- tile_count: int32 [4, 8], P('row', 'col'), may hold values from 1 to 8, as said below
- weight: bfloat16 [1024, 512], replicated, may hold values from -0.25 to 0.25
- cotangent: bfloat16 [4096, 512], P(('row', 'col')), may hold values from -6 to 6
Outputs:
- hidden: bfloat16 [4096, 512], P(('row', 'col'))
- weight_grad: float32 [1024, 512], replicated
The draws below stay inside these ranges and needn't reach their ends.
Inputs may be any that keep to these rules, and one draw needn't show every extreme that they name: `tile_count`: some device has all 8 slots live. `tile_rows`: every slot of device (r, c) names tile row (c + k) mod 8 with 0 <= k < 4; slot 0 of every device has k = 3.
All inputs are finite; a program needn't handle non-finite values.
Results may differ from the reference program's by a relative error of at most 0.0035.
Values may be sent and summed in bfloat16 or wider, within the bound.
A program may use at most 64 MiB of HBM per device.

```python
import jax
import jax.numpy as jnp
from jax import lax

F = 512
TILE = 128
REACH = 4
TPD = 8
NPD = 128
NODES = 4096
RB = 8
CB = 4
N_ROW = 4
N_COL = 8


def draw_tile_count(key, part):
    counts = jax.random.randint(key, (N_ROW * N_COL,), 1, TPD + 1)
    chosen = jax.random.randint(jax.random.fold_in(key, 7), (), 0, N_ROW * N_COL)
    counts = jnp.where(jnp.arange(N_ROW * N_COL) == chosen, TPD, counts)
    return counts.reshape(N_ROW, N_COL).astype(jnp.int32)


def draw_tile_rows(key, part):
    slots = jnp.arange(N_COL * TPD, dtype=jnp.int32)
    owner = slots // TPD
    offsets = jax.random.randint(key, (N_ROW, N_COL * TPD), 0, REACH)
    offsets = jnp.where((slots % TPD == 0)[None, :], REACH - 1, offsets)
    return ((owner[None, :] + offsets) % N_COL).astype(jnp.int32)


def with_ends(values, own_key, low, top_value):
    index_at = [jax.random.randint(jax.random.fold_in(own_key, axis), (), 0, length) for axis, length in enumerate(values.shape)]
    widest = values.shape.index(max(values.shape))
    next_to = index_at[:widest] + [(index_at[widest] + 1) % values.shape[widest]] + index_at[widest + 1:]
    return values.at[tuple(index_at)].set(low).at[tuple(next_to)].set(top_value)


def shard_levels(rng, dims, pieces, least, top_value):
    def one(axis_at, blocks):
        draws = jax.random.uniform(jax.random.fold_in(jax.random.fold_in(rng, 6), axis_at), (blocks,), jnp.float32, least / len(pieces), top_value / len(pieces))
        return jnp.repeat(jnp.exp(draws), dims[axis_at] // blocks).reshape((-1,) + (1,) * (len(dims) - axis_at - 1))

    factor_of = one(*pieces[0])
    for cut in pieces[1:]:
        factor_of = factor_of * one(*cut)
    return factor_of


def noise(own_key, dims, scale, limit, cuts=(), kind=jnp.bfloat16):
    loudness = shard_levels(own_key, dims, cuts, -0.22, 0.18) if cuts else 1.0
    entries = jax.random.normal(own_key, dims, jnp.float32) * scale * loudness
    return jnp.minimum(jnp.maximum(entries, -limit), limit).astype(kind)


def setup_inputs(seed: int = 0) -> dict:
    seeds = jax.random.split(jax.random.key(seed), 8)
    return {
        "features": noise(seeds[0], (NODES, F), 1.0, 6.0, ((0, 32),)),
        "adj_tiles": noise(seeds[1], (N_ROW, N_COL * TPD, TILE, TILE), (TPD * TILE * TILE // NPD) ** -0.5, 0.1875, ((0, 4), (1, 8))),
        "tile_rows": draw_tile_rows(jax.random.fold_in(seeds[7], 71), 0),
        "tile_cols": with_ends(jax.random.randint(seeds[3], (N_ROW, N_COL * TPD), 0, CB), jax.random.fold_in(seeds[3], 1), 0, CB - 1).astype(jnp.int32),
        "tile_count": draw_tile_count(jax.random.fold_in(seeds[7], 71), 0),
        "weight": noise(seeds[5], (2 * F, F), F ** -0.5, 0.25),
        "cotangent": noise(seeds[6], (NODES, F), 1.0, 6.0, ((0, 32),)),
    }


def tile_forward(adj_tiles, rows_idx, cols_idx, count, source, num_rows):
    width = source.shape[1]
    blocks = source.reshape(-1, TILE, width)
    chosen = jnp.take(blocks, cols_idx, axis=0).astype(jnp.float32)
    products = jnp.einsum('tij,tjx->tix', adj_tiles.astype(jnp.float32), chosen, precision=lax.Precision.HIGHEST)
    live_mask = (jnp.arange(adj_tiles.shape[0]) < count).astype(jnp.float32)
    placing = (rows_idx[:, None] == jnp.arange(num_rows)[None, :]).astype(jnp.float32) * live_mask[:, None]
    total = jnp.einsum('tr,tix->rix', placing, products, precision=lax.Precision.HIGHEST)
    return total.reshape(num_rows * TILE, width)


def tile_backward(adj_tiles, rows_idx, cols_idx, count, source, num_cols):
    width = source.shape[1]
    blocks = source.reshape(-1, TILE, width)
    chosen = jnp.take(blocks, rows_idx, axis=0).astype(jnp.float32)
    products = jnp.einsum('tji,tjx->tix', adj_tiles.astype(jnp.float32), chosen, precision=lax.Precision.HIGHEST)
    live_mask = (jnp.arange(adj_tiles.shape[0]) < count).astype(jnp.float32)
    placing = (cols_idx[:, None] == jnp.arange(num_cols)[None, :]).astype(jnp.float32) * live_mask[:, None]
    total = jnp.einsum('tc,tix->cix', placing, products, precision=lax.Precision.HIGHEST)
    return total.reshape(num_cols * TILE, width)


def reference(features, adj_tiles, tile_rows, tile_cols, tile_count, weight, cotangent):
    width = features.shape[1]
    total_nodes = features.shape[0]
    w_self = weight[:width]
    w_neigh = weight[width:]
    projected = jnp.dot(features, w_neigh, preferred_element_type=jnp.float32).astype(jnp.bfloat16)
    col_proj = projected.reshape(N_ROW, N_COL, NPD, width).transpose(1, 0, 2, 3).reshape(N_COL, N_ROW * NPD, width)
    col_feats = features.reshape(N_ROW, N_COL, NPD, width).transpose(1, 0, 2, 3).reshape(N_COL, N_ROW * NPD, width)
    grid_tiles = adj_tiles.reshape(N_ROW, N_COL, TPD, TILE, TILE)
    grid_rows = tile_rows.reshape(N_ROW, N_COL, TPD)
    grid_cols = tile_cols.reshape(N_ROW, N_COL, TPD)

    def row_slab(row_idx):
        def step(total, col_idx):
            part = tile_forward(grid_tiles[row_idx, col_idx], grid_rows[row_idx, col_idx], grid_cols[row_idx, col_idx],
                                tile_count[row_idx, col_idx], col_proj[col_idx], RB)
            return total + part, None
        total, _ = lax.scan(step, jnp.zeros((RB * TILE, width), jnp.float32), jnp.arange(N_COL, dtype=jnp.int32))
        return total

    neighbour = lax.map(row_slab, jnp.arange(N_ROW, dtype=jnp.int32)).reshape(total_nodes, width)
    pre_act = jnp.dot(features, w_self, preferred_element_type=jnp.float32) + neighbour
    hidden = jax.nn.silu(pre_act).astype(jnp.bfloat16)
    sigmoid_z = jax.nn.sigmoid(pre_act)
    slope = sigmoid_z * (1.0 + pre_act * (1.0 - sigmoid_z))
    upstream = (cotangent.astype(jnp.float32) * slope).astype(jnp.bfloat16)
    grad_self = jnp.dot(features.T, upstream, preferred_element_type=jnp.float32)
    row_up = upstream.reshape(N_ROW, N_COL * NPD, width)

    def back(total, device_idx):
        row_idx = device_idx // N_COL
        col_idx = device_idx % N_COL
        spread = tile_backward(grid_tiles[row_idx, col_idx], grid_rows[row_idx, col_idx], grid_cols[row_idx, col_idx],
                               tile_count[row_idx, col_idx], row_up[row_idx], CB)
        term = jnp.dot(col_feats[col_idx].astype(jnp.float32).T, spread, precision=lax.Precision.HIGHEST)
        return total + term, None

    grad_neigh, _ = lax.scan(back, jnp.zeros((width, width), jnp.float32), jnp.arange(N_ROW * N_COL, dtype=jnp.int32))
    weight_grad = jnp.concatenate([grad_self, grad_neigh], axis=0) * (float(total_nodes) ** -0.5)
    return hidden, weight_grad
```

```python
import jax
import jax.numpy as jnp
from jax import lax
from jax.sharding import PartitionSpec as P

REACH = 4


def from_behind(value, axis, steps):
    count = lax.axis_size(axis)
    pairs = [(source, (source + steps) % count) for source in range(count)]
    return lax.ppermute(value, axis, pairs)


def split(value):
    high = value.astype(jnp.bfloat16)
    return high, (value - high.astype(jnp.float32)).astype(jnp.bfloat16)


def dot(a, b):
    return jnp.dot(a, b, preferred_element_type=jnp.float32)


def body(features, adj_tiles, tile_rows, tile_cols, tile_count, weight, cotangent):
    width = features.shape[1]
    own_nodes = features.shape[0]
    row_count = lax.axis_size("row")
    col_count = lax.axis_size("col")
    tiles = adj_tiles[0]
    slots, size = tiles.shape[:2]
    position = lax.axis_index("col")
    offsets = (tile_rows[0] - position) % col_count
    live = jnp.arange(slots) < tile_count[0, 0]
    col_feats = lax.all_gather(features, "row", axis=0, tiled=True)
    chosen = jnp.take(col_feats.reshape(-1, size, width), tile_cols[0], axis=0).reshape(slots * size, width)
    placed = (offsets[None, :] == jnp.arange(REACH)[:, None]) & live[None, :]
    masked = jnp.where(placed[:, None, :, None], tiles.transpose(1, 0, 2)[None], 0)
    sums = dot(masked.reshape(REACH * size, slots * size), chosen).reshape(REACH, size, width)
    total = sums[0]
    for step in range(1, REACH):
        total = total + from_behind(sums[step], "col", step)
    high, low = split(total)
    pre_act = dot(features, weight[:width]) + dot(high, weight[width:]) + dot(low, weight[width:])
    hidden = jax.nn.silu(pre_act).astype(jnp.bfloat16)
    sigmoid_z = jax.nn.sigmoid(pre_act)
    slope = sigmoid_z * (1.0 + pre_act * (1.0 - sigmoid_z))
    upstream = (cotangent.astype(jnp.float32) * slope).astype(jnp.bfloat16)
    grad_self = dot(features.T, upstream)
    grad_neigh = dot(high.T, upstream) + dot(low.T, upstream)
    stacked = jnp.concatenate([grad_self, grad_neigh], axis=0)
    summed = lax.psum(stacked, ("row", "col"))
    total_nodes = own_nodes * row_count * col_count
    return hidden, summed * float(total_nodes) ** (-0.5)


def solution(mesh):
    in_specs = (
        P(("row", "col"), None),
        P("row", "col", None, None),
        P("row", "col"),
        P("row", "col"),
        P("row", "col"),
        P(),
        P(("row", "col"), None),
    )
    out_specs = (P(("row", "col"), None), P())
    return jax.shard_map(body, mesh=mesh, in_specs=in_specs, out_specs=out_specs, check_vma=False)
```

```python
import functools

import jax
import jax.numpy as jnp
from jax import lax
from jax.experimental import pallas as pl
from jax.experimental.pallas import tpu as pltpu
from jax.sharding import PartitionSpec as P

REACH = 4


def from_behind(value, axis, steps):
    count = lax.axis_size(axis)
    pairs = [(source, (source + steps) % count) for source in range(count)]
    return lax.ppermute(value, axis, pairs)


def split(value):
    high = value.astype(jnp.bfloat16)
    return high, (value - high.astype(jnp.float32)).astype(jnp.bfloat16)


def dot(a, b):
    return jnp.dot(a, b, preferred_element_type=jnp.float32)


MESH = pl.DeviceIdType.MESH


def kernel(n_row, n_col, scale, features, tiles, rows, cols, count, weight, cotangent, hidden, grad,
           slab, chosen, part, arrived, left_high, left_low, give, taken, up_give, up_taken,
           term, term_in, piece, piece_in, own_part, self_part, send, recv):
    r, c = lax.axis_index("row"), lax.axis_index("col")
    core, z = lax.rem(c, 2), lax.div(c, 2)
    n_z = n_col // 2
    size, width = features.shape
    slots = tiles.shape[0]
    sibling = (r, c + 1 - 2 * core)
    counter = iter(range(1000))

    def copy(source, target, landing, device):
        slot = next(counter)
        out = pltpu.make_async_remote_copy(source, target, send.at[slot], recv.at[slot], device, MESH)
        into = pltpu.make_async_remote_copy(landing, landing, send.at[slot], recv.at[slot], device, MESH)
        return out, into

    barrier = pltpu.get_barrier_semaphore()
    row_peers = [(lax.rem(r + d, n_row), c) for d in range(1, n_row)]
    col_peers = [(r, lax.rem(c + d, n_col)) for d in range(1, n_col)]
    for peer in row_peers + col_peers:
        pl.semaphore_signal(barrier, inc=1, device_id=peer, device_id_type=MESH)
    pl.semaphore_wait(barrier, len(row_peers) + len(col_peers))

    sent = []

    def start(out):
        out.start()
        sent.append(out)

    gathers = []
    for d in range(1, n_row):
        out, into = copy(features, slab.at[r], slab.at[lax.rem(r + n_row - d, n_row)], (lax.rem(r + d, n_row), c))
        start(out)
        gathers.append(into)
    slab[r] = features[...]
    self_part[...] = dot(features[...], weight[:width])
    for into in gathers:
        into.wait_recv()

    for s in range(slots):
        chosen[s * size:(s + 1) * size, :] = slab[cols[0, s]]
    live = count[0, 0]
    offsets = [lax.rem(rows[0, s] - c + n_col, n_col) for s in range(slots)]

    def block_sum(k):
        masked = [
            jnp.where(jnp.logical_and(offsets[s] == k, s < live), tiles[s], jnp.zeros_like(tiles[s]))
            for s in range(slots)
        ]
        return dot(jnp.concatenate(masked, axis=1), chosen[...])

    incoming = []
    for k in range(REACH - 1, 0, -1):
        part[k - 1] = block_sum(k).astype(jnp.bfloat16)
        out, into = copy(part.at[k - 1], arrived.at[k - 1], arrived.at[k - 1], (r, lax.rem(c + k, n_col)))
        start(out)
        incoming.append(into)
    own_part[...] = block_sum(0)
    total = own_part[...]
    for k, into in zip(range(REACH - 1, 0, -1), incoming):
        into.wait_recv()
        total = total + arrived[k - 1].astype(jnp.float32)

    high, low = split(total)
    first = core == 0
    empty = jnp.zeros_like(high)
    give[0] = jnp.where(first, high, features[...])
    give[1] = jnp.where(first, low, empty)
    out, lefts = copy(give, taken, taken, sibling)
    start(out)
    left_high[:, :size] = jnp.where(first, features[...], high).T
    left_low[:, :size] = jnp.where(first, empty, low).T

    pre_act = self_part[...] + dot(high, weight[width:]) + dot(low, weight[width:])
    gate = 1.0 / (1.0 + jnp.exp(-pre_act))
    hidden[...] = (pre_act * gate).astype(jnp.bfloat16)
    slope = gate * (1.0 + pre_act * (1.0 - gate))
    up_give[...] = (cotangent[...].astype(jnp.float32) * slope).astype(jnp.bfloat16)
    out, ups = copy(up_give, up_taken, up_taken, sibling)
    start(out)
    lefts.wait_recv()
    left_high[:, size:] = taken[0].T
    left_low[:, size:] = taken[1].T
    ups.wait_recv()
    upstream = jnp.concatenate([up_give[...], up_taken[...]], axis=0)

    share = width // n_row
    small = share // n_z

    def rows_of(q):
        at = pl.ds(pl.multiple_of(q * share, share), share)
        return dot(left_high[at, :], upstream) + dot(left_low[at, :], upstream)

    incoming = []
    for d in range(1, n_row):
        q = lax.rem(r + d, n_row)
        term[d - 1] = rows_of(q).astype(jnp.bfloat16)
        out, into = copy(term.at[d - 1], term_in.at[d - 1], term_in.at[d - 1], (q, c))
        start(out)
        incoming.append(into)
    total = rows_of(r)
    for d, into in enumerate(incoming):
        into.wait_recv()
        total = total + term_in[d].astype(jnp.float32)
    piece[...] = total
    incoming = []
    for d in range(1, n_z):
        q = lax.rem(z + d, n_z)
        at = pl.ds(pl.multiple_of(q * small, small), small)
        out, into = copy(piece.at[at], piece_in.at[d - 1], piece_in.at[d - 1], (r, 2 * q + core))
        start(out)
        incoming.append(into)
    total = piece[pl.ds(pl.multiple_of(z * small, small), small), :]
    for d, into in enumerate(incoming):
        into.wait_recv()
        total = total + piece_in[d]

    def region(half, q, level):
        return grad.at[pl.ds(pl.multiple_of(half * width + q * share + level * small, small), small)]

    def band(half, q):
        return grad.at[pl.ds(pl.multiple_of(half * width + q * share, share), share)]

    mine = region(core, r, z)
    mine[...] = (total * scale).astype(jnp.bfloat16)
    incoming = []
    for d in range(1, n_z):
        q = lax.rem(z + d, n_z)
        out, into = copy(mine, mine, region(core, r, lax.rem(z + n_z - d, n_z)), (r, 2 * q + core))
        start(out)
        incoming.append(into)
    for into in incoming:
        into.wait_recv()
    incoming = []
    mine = band(core, r)
    for d in range(1, n_row):
        out, into = copy(mine, mine, band(core, lax.rem(r + n_row - d, n_row)), (lax.rem(r + d, n_row), c))
        start(out)
        incoming.append(into)
    last = []
    for d in range(n_row):
        q = lax.rem(r + n_row - d, n_row)
        if d > 0:
            incoming[d - 1].wait_recv()
        out, into = copy(band(core, q), band(core, q), band(1 - core, q), sibling)
        start(out)
        last.append(into)
    for into in last:
        into.wait_recv()
    for out in sent:
        out.wait_send()


def fused(features, tiles, rows, cols, count, weight, cotangent, n_row, n_col):
    size, width = features.shape
    slots = tiles.shape[0]
    share = width // n_row
    small = share // (n_col // 2)
    half, full = jnp.bfloat16, jnp.float32
    copies = 3 * (n_row - 1) + (REACH - 1) + 2 * (n_col // 2 - 1) + 2 + n_row
    vmem = pl.BlockSpec(memory_space=pltpu.VMEM)
    smem = pl.BlockSpec(memory_space=pltpu.SMEM)
    return pl.pallas_call(
        functools.partial(kernel, n_row, n_col, float(size * n_row * n_col) ** (-0.5)),
        out_shape=(
            jax.ShapeDtypeStruct((size, width), half),
            jax.ShapeDtypeStruct((2 * width, width), half),
        ),
        in_specs=[vmem, vmem, smem, smem, smem, vmem, vmem],
        out_specs=(vmem, vmem),
        scratch_shapes=[
            pltpu.VMEM((n_row, size, width), half),
            pltpu.VMEM((slots * size, width), half),
            pltpu.VMEM((REACH - 1, size, width), half),
            pltpu.VMEM((REACH - 1, size, width), half),
            pltpu.VMEM((width, 2 * size), half),
            pltpu.VMEM((width, 2 * size), half),
            pltpu.VMEM((2, size, width), half),
            pltpu.VMEM((2, size, width), half),
            pltpu.VMEM((size, width), half),
            pltpu.VMEM((size, width), half),
            pltpu.VMEM((n_row - 1, share, width), half),
            pltpu.VMEM((n_row - 1, share, width), half),
            pltpu.VMEM((share, width), full),
            pltpu.VMEM((n_col // 2 - 1, small, width), full),
            pltpu.VMEM((size, width), full),
            pltpu.VMEM((size, width), full),
            pltpu.SemaphoreType.DMA((copies,)),
            pltpu.SemaphoreType.DMA((copies,)),
        ],
        compiler_params=pltpu.CompilerParams(
            collective_id=0, has_side_effects=True, vmem_limit_bytes=40 * 1024 * 1024
        ),
    )(features, tiles, rows, cols, count, weight, cotangent)


def body(features, adj_tiles, tile_rows, tile_cols, tile_count, weight, cotangent):
    width = features.shape[1]
    own_nodes = features.shape[0]
    row_count = lax.axis_size("row")
    col_count = lax.axis_size("col")
    tiles = adj_tiles[0]
    slots, size = tiles.shape[:2]
    share = width // row_count
    small = share // (col_count // 2)
    if col_count % 2 == 0 and REACH <= col_count and small >= 16 and small % 16 == 0:
        hidden, grad = fused(
            features, tiles, tile_rows, tile_cols, tile_count, weight, cotangent, row_count, col_count
        )
        return hidden, grad.astype(jnp.float32)
    position = lax.axis_index("col")
    offsets = (tile_rows[0] - position) % col_count
    live = jnp.arange(slots) < tile_count[0, 0]
    col_feats = lax.all_gather(features, "row", axis=0, tiled=True)
    chosen = jnp.take(col_feats.reshape(-1, size, width), tile_cols[0], axis=0).reshape(slots * size, width)
    placed = (offsets[None, :] == jnp.arange(REACH)[:, None]) & live[None, :]
    masked = jnp.where(placed[:, None, :, None], tiles.transpose(1, 0, 2)[None], 0)
    sums = dot(masked.reshape(REACH * size, slots * size), chosen).reshape(REACH, size, width)
    total = sums[0]
    for step in range(1, REACH):
        total = total + from_behind(sums[step], "col", step)
    high, low = split(total)
    pre_act = dot(features, weight[:width]) + dot(high, weight[width:]) + dot(low, weight[width:])
    hidden = jax.nn.silu(pre_act).astype(jnp.bfloat16)
    sigmoid_z = jax.nn.sigmoid(pre_act)
    slope = sigmoid_z * (1.0 + pre_act * (1.0 - sigmoid_z))
    upstream = (cotangent.astype(jnp.float32) * slope).astype(jnp.bfloat16)
    grad_self = dot(features.T, upstream)
    grad_neigh = dot(high.T, upstream) + dot(low.T, upstream)
    stacked = jnp.concatenate([grad_self, grad_neigh], axis=0)
    summed = lax.psum(stacked, ("row", "col"))
    total_nodes = own_nodes * row_count * col_count
    return hidden, summed * float(total_nodes) ** (-0.5)


def solution(mesh):
    in_specs = (
        P(("row", "col"), None),
        P("row", "col", None, None),
        P("row", "col"),
        P("row", "col"),
        P("row", "col"),
        P(),
        P(("row", "col"), None),
    )
    out_specs = (P(("row", "col"), None), P())
    return jax.shard_map(body, mesh=mesh, in_specs=in_specs, out_specs=out_specs, check_vma=False)
```

```python
import functools

import jax
import jax.numpy as jnp
from jax import lax
from jax.experimental import pallas as pl
from jax.experimental.pallas import tpu as pltpu
from jax.sharding import PartitionSpec as P

REACH = 4


def from_behind(value, axis, steps):
    count = lax.axis_size(axis)
    pairs = [(source, (source + steps) % count) for source in range(count)]
    return lax.ppermute(value, axis, pairs)


def split(value):
    high = value.astype(jnp.bfloat16)
    return high, (value - high.astype(jnp.float32)).astype(jnp.bfloat16)


def dot(a, b):
    return jnp.dot(a, b, preferred_element_type=jnp.float32)


MESH = pl.DeviceIdType.MESH
PARTS = 2


def kernel(n_row, n_col, scale, features, tiles_in, rows, cols, count, weight_in, cotangent_in, hidden_out, grad_out,
           tiles, weight, cotangent, hidden, grad, masked, chosen, part, arrived, left_high, left_low,
           give, taken, up_give, up_taken, term, term_in, piece, piece_in, own_part, self_part, send, recv, local, *slabs):
    r, c = lax.axis_index("row"), lax.axis_index("col")
    core, z = lax.rem(c, 2), lax.div(c, 2)
    n_z = n_col // 2
    size, width = features.shape
    slots = tiles.shape[0]
    wide = width // PARTS
    sibling = (r, c + 1 - 2 * core)
    counter = iter(range(1000))
    local_counter = iter(range(1000))

    def copy(source, target, landing, device):
        slot = next(counter)
        out = pltpu.make_async_remote_copy(source, target, send.at[slot], recv.at[slot], device, MESH)
        into = pltpu.make_async_remote_copy(landing, landing, send.at[slot], recv.at[slot], device, MESH)
        return out, into

    def bring(source, target):
        moved = pltpu.make_async_copy(source, target, local.at[next(local_counter)])
        moved.start()
        return moved

    def columns(p):
        return pl.ds(p * wide, wide)

    barrier = pltpu.get_barrier_semaphore()
    row_peers = [(lax.rem(r + d, n_row), c) for d in range(1, n_row)]
    col_peers = [(r, lax.rem(c + d, n_col)) for d in range(1, n_col)]
    for peer in row_peers + col_peers:
        pl.semaphore_signal(barrier, inc=1, device_id=peer, device_id_type=MESH)
    own_feats = [bring(features.at[:, columns(p)], slabs[p].at[r]) for p in range(PARTS)]
    tiles_here = bring(tiles_in, tiles)
    weight_here = bring(weight_in, weight)
    cotangent_here = bring(cotangent_in, cotangent)
    pl.semaphore_wait(barrier, len(row_peers) + len(col_peers))

    sent = []

    def start(out):
        out.start()
        sent.append(out)

    gathers = []
    for p in range(PARTS):
        gathers.append([])
        for d in range(1, n_row):
            out, into = copy(features.at[:, columns(p)], slabs[p].at[r],
                             slabs[p].at[lax.rem(r + n_row - d, n_row)], (lax.rem(r + d, n_row), c))
            start(out)
            gathers[p].append(into)

    live = count[0, 0]
    offsets = [lax.rem(rows[0, s] - c + n_col, n_col) for s in range(slots)]
    tiles_here.wait()
    for k in range(REACH):
        for s in range(slots):
            masked[k, :, s * size:(s + 1) * size] = jnp.where(
                jnp.logical_and(offsets[s] == k, s < live), tiles[s], jnp.zeros_like(tiles[s])
            )
    for moved in own_feats:
        moved.wait()
    weight_here.wait()
    feats = jnp.concatenate([slabs[p][r] for p in range(PARTS)], axis=1)
    self_part[...] = dot(feats, weight[:width])
    cotangent_here.wait()

    sums = []
    for p in range(PARTS):
        for into in gathers[p]:
            into.wait_recv()
        for s in range(slots):
            chosen[p, s * size:(s + 1) * size, :] = slabs[p][cols[0, s]]
        sums.append([])
        for k in range(REACH - 1, 0, -1):
            part[p, k - 1] = dot(masked[k], chosen[p]).astype(jnp.bfloat16)
            out, into = copy(part.at[p, k - 1], arrived.at[p, k - 1], arrived.at[p, k - 1], (r, lax.rem(c + k, n_col)))
            start(out)
            sums[p].append((k, into))
        own_part[p] = dot(masked[0], chosen[p])

    first = core == 0
    lefts = []
    highs, lows = [], []
    for p in range(PARTS):
        total = own_part[p]
        for k, into in sums[p]:
            into.wait_recv()
            total = total + arrived[p, k - 1].astype(jnp.float32)
        high, low = split(total)
        highs.append(high)
        lows.append(low)
        mine = slabs[p][r]
        empty = jnp.zeros_like(high)
        give[p, 0] = jnp.where(first, high, mine)
        give[p, 1] = jnp.where(first, low, empty)
        out, into = copy(give.at[p], taken.at[p], taken.at[p], sibling)
        start(out)
        lefts.append(into)
        left_high[p * wide:(p + 1) * wide, :size] = jnp.where(first, mine, high).T
        left_low[p * wide:(p + 1) * wide, :size] = jnp.where(first, empty, low).T

    high = jnp.concatenate(highs, axis=1)
    low = jnp.concatenate(lows, axis=1)
    ups = []
    for p in range(PARTS):
        at = slice(p * wide, (p + 1) * wide)
        pre_act = self_part[:, at] + dot(high, weight[width:, at]) + dot(low, weight[width:, at])
        gate = 1.0 / (1.0 + jnp.exp(-pre_act))
        slope = gate * (1.0 + pre_act * (1.0 - gate))
        up_give[p] = (cotangent[:, at].astype(jnp.float32) * slope).astype(jnp.bfloat16)
        out, into = copy(up_give.at[p], up_taken.at[p], up_taken.at[p], sibling)
        start(out)
        ups.append(into)
        hidden[:, at] = (pre_act * gate).astype(jnp.bfloat16)
    placed = [bring(hidden, hidden_out)]
    for p in range(PARTS):
        lefts[p].wait_recv()
        left_high[p * wide:(p + 1) * wide, size:] = taken[p, 0].T
        left_low[p * wide:(p + 1) * wide, size:] = taken[p, 1].T

    share = width // n_row
    small = share // n_z

    def block(half, q, level, p):
        return grad.at[pl.ds(pl.multiple_of(half * width + q * share + level * small, small), small), columns(p)]

    def band(half, q, p):
        return grad.at[pl.ds(pl.multiple_of(half * width + q * share, share), share), columns(p)]

    waiting = []
    for p in range(PARTS):
        ups[p].wait_recv()
        upstream = jnp.concatenate([up_give[p], up_taken[p]], axis=0)
        waiting.append([])
        for d in range(n_row - 1, -1, -1):
            q = lax.rem(r + d, n_row)
            at = pl.ds(pl.multiple_of(q * share, share), share)
            value = dot(left_high[at, :], upstream) + dot(left_low[at, :], upstream)
            if d == 0:
                piece[p] = value
                continue
            term[p, d - 1] = value.astype(jnp.bfloat16)
            out, into = copy(term.at[p, d - 1], term_in.at[p, d - 1], term_in.at[p, d - 1], (q, c))
            start(out)
            waiting[p].append((d, into))
    over_z = []
    for p in range(PARTS):
        total = piece[p]
        for d, into in waiting[p]:
            into.wait_recv()
            total = total + term_in[p, d - 1].astype(jnp.float32)
        piece[p] = total
        over_z.append([])
        for d in range(1, n_z):
            q = lax.rem(z + d, n_z)
            at = pl.ds(pl.multiple_of(q * small, small), small)
            out, into = copy(piece.at[p, at], piece_in.at[p, d - 1], piece_in.at[p, d - 1], (r, 2 * q + core))
            start(out)
            over_z[p].append((d, into))

    back_z = []
    for p in range(PARTS):
        total = piece[p, pl.ds(pl.multiple_of(z * small, small), small), :]
        for d, into in over_z[p]:
            into.wait_recv()
            total = total + piece_in[p, d - 1]
        mine = block(core, r, z, p)
        mine[...] = (total * scale).astype(jnp.bfloat16)
        back_z.append([])
        for d in range(1, n_z):
            out, into = copy(mine, mine, block(core, r, lax.rem(z + n_z - d, n_z), p),
                             (r, 2 * lax.rem(z + d, n_z) + core))
            start(out)
            back_z[p].append(into)
    back_row = []
    last = []

    def pass_on(q, p):
        out, into = copy(band(core, q, p), band(core, q, p), band(1 - core, q, p), sibling)
        start(out)
        last.append((into, q, p))

    for p in range(PARTS):
        for into in back_z[p]:
            into.wait_recv()
        mine = band(core, r, p)
        back_row.append([])
        for d in range(1, n_row):
            q = lax.rem(r + n_row - d, n_row)
            out, into = copy(mine, mine, band(core, q, p), (lax.rem(r + d, n_row), c))
            start(out)
            back_row[p].append((q, into))
        pass_on(r, p)
    for p in range(PARTS):
        for q, into in back_row[p]:
            into.wait_recv()
            pass_on(q, p)
    half = pl.ds(pl.multiple_of(core * width, width), width)
    placed.append(bring(grad.at[half], grad_out.at[half]))
    for into, q, p in last:
        into.wait_recv()
    half = pl.ds(pl.multiple_of((1 - core) * width, width), width)
    placed.append(bring(grad.at[half], grad_out.at[half]))
    for moved in placed:
        moved.wait()
    for out in sent:
        out.wait_send()


def fused(features, tiles, rows, cols, count, weight, cotangent, n_row, n_col):
    size, width = features.shape
    slots = tiles.shape[0]
    wide = width // PARTS
    share = width // n_row
    n_z = n_col // 2
    small = share // n_z
    half, full = jnp.bfloat16, jnp.float32
    copies = PARTS * (3 * (n_row - 1) + (REACH - 1) + 2 * (n_z - 1) + 2 + n_row)
    hbm = pl.BlockSpec(memory_space=pl.ANY)
    smem = pl.BlockSpec(memory_space=pltpu.SMEM)
    return pl.pallas_call(
        functools.partial(kernel, n_row, n_col, float(size * n_row * n_col) ** (-0.5)),
        out_shape=(
            jax.ShapeDtypeStruct((size, width), half),
            jax.ShapeDtypeStruct((2 * width, width), half),
        ),
        in_specs=[hbm, hbm, smem, smem, smem, hbm, hbm],
        out_specs=(hbm, hbm),
        scratch_shapes=[
            pltpu.VMEM(tiles.shape, half),
            pltpu.VMEM(weight.shape, half),
            pltpu.VMEM((size, width), half),
            pltpu.VMEM((size, width), half),
            pltpu.VMEM((2 * width, width), half),
            pltpu.VMEM((REACH, size, slots * size), half),
            pltpu.VMEM((PARTS, slots * size, wide), half),
            pltpu.VMEM((PARTS, REACH - 1, size, wide), half),
            pltpu.VMEM((PARTS, REACH - 1, size, wide), half),
            pltpu.VMEM((width, 2 * size), half),
            pltpu.VMEM((width, 2 * size), half),
            pltpu.VMEM((PARTS, 2, size, wide), half),
            pltpu.VMEM((PARTS, 2, size, wide), half),
            pltpu.VMEM((PARTS, size, wide), half),
            pltpu.VMEM((PARTS, size, wide), half),
            pltpu.VMEM((PARTS, n_row - 1, share, wide), half),
            pltpu.VMEM((PARTS, n_row - 1, share, wide), half),
            pltpu.VMEM((PARTS, share, wide), full),
            pltpu.VMEM((PARTS, n_z - 1, small, wide), full),
            pltpu.VMEM((PARTS, size, wide), full),
            pltpu.VMEM((size, width), full),
            pltpu.SemaphoreType.DMA((copies,)),
            pltpu.SemaphoreType.DMA((copies,)),
            pltpu.SemaphoreType.DMA((PARTS + 6,)),
            *[pltpu.VMEM((n_row, size, wide), half)] * PARTS,
        ],
        compiler_params=pltpu.CompilerParams(
            collective_id=0, has_side_effects=True, vmem_limit_bytes=60 * 1024 * 1024
        ),
    )(features, tiles, rows, cols, count, weight, cotangent)


def body(features, adj_tiles, tile_rows, tile_cols, tile_count, weight, cotangent):
    width = features.shape[1]
    own_nodes = features.shape[0]
    row_count = lax.axis_size("row")
    col_count = lax.axis_size("col")
    tiles = adj_tiles[0]
    slots, size = tiles.shape[:2]
    share = width // row_count
    small = share // (col_count // 2)
    if col_count % 2 == 0 and REACH <= col_count and small >= 16 and small % 16 == 0:
        hidden, grad = fused(
            features, tiles, tile_rows, tile_cols, tile_count, weight, cotangent, row_count, col_count
        )
        return hidden, grad.astype(jnp.float32)
    position = lax.axis_index("col")
    offsets = (tile_rows[0] - position) % col_count
    live = jnp.arange(slots) < tile_count[0, 0]
    col_feats = lax.all_gather(features, "row", axis=0, tiled=True)
    chosen = jnp.take(col_feats.reshape(-1, size, width), tile_cols[0], axis=0).reshape(slots * size, width)
    placed = (offsets[None, :] == jnp.arange(REACH)[:, None]) & live[None, :]
    masked = jnp.where(placed[:, None, :, None], tiles.transpose(1, 0, 2)[None], 0)
    sums = dot(masked.reshape(REACH * size, slots * size), chosen).reshape(REACH, size, width)
    total = sums[0]
    for step in range(1, REACH):
        total = total + from_behind(sums[step], "col", step)
    high, low = split(total)
    pre_act = dot(features, weight[:width]) + dot(high, weight[width:]) + dot(low, weight[width:])
    hidden = jax.nn.silu(pre_act).astype(jnp.bfloat16)
    sigmoid_z = jax.nn.sigmoid(pre_act)
    slope = sigmoid_z * (1.0 + pre_act * (1.0 - sigmoid_z))
    upstream = (cotangent.astype(jnp.float32) * slope).astype(jnp.bfloat16)
    grad_self = dot(features.T, upstream)
    grad_neigh = dot(high.T, upstream) + dot(low.T, upstream)
    stacked = jnp.concatenate([grad_self, grad_neigh], axis=0)
    summed = lax.psum(stacked, ("row", "col"))
    total_nodes = own_nodes * row_count * col_count
    return hidden, summed * float(total_nodes) ** (-0.5)


def solution(mesh):
    in_specs = (
        P(("row", "col"), None),
        P("row", "col", None, None),
        P("row", "col"),
        P("row", "col"),
        P("row", "col"),
        P(),
        P(("row", "col"), None),
    )
    out_specs = (P(("row", "col"), None), P())
    return jax.shard_map(body, mesh=mesh, in_specs=in_specs, out_specs=out_specs, check_vma=False)
```

```python
import functools

import jax
import jax.numpy as jnp
from jax import lax
from jax.experimental import pallas as pl
from jax.experimental.pallas import tpu as pltpu
from jax.sharding import PartitionSpec as P

REACH = 4


def from_behind(value, axis, steps):
    count = lax.axis_size(axis)
    pairs = [(source, (source + steps) % count) for source in range(count)]
    return lax.ppermute(value, axis, pairs)


def split(value):
    high = value.astype(jnp.bfloat16)
    return high, (value - high.astype(jnp.float32)).astype(jnp.bfloat16)


def dot(a, b):
    return jnp.dot(a, b, preferred_element_type=jnp.float32)


MESH = pl.DeviceIdType.MESH
PARTS = 2


def flip(index, bits):
    for bit in (1, 2, 4, 8, 16):
        if bits & bit:
            index = index + bit - 2 * bit * lax.rem(lax.div(index, bit), 2)
    return index


def kernel(n_row, n_col, scale, features, tiles_in, rows, cols, count, weight_in, cotangent_in, hidden, grad_out,
           tiles, weight, cotangent, grad, wide_grad, masked, chosen, part, arrived, swap, swap_in, left_high, left_low,
           give, taken, up_give, up_taken, term, term_in, piece, near_in, far, far_in, own_part, self_part, send, recv, local, *slabs):
    r, c = lax.axis_index("row"), lax.axis_index("col")
    core, z = lax.rem(c, 2), lax.div(c, 2)
    n_z = n_col // 2
    size, width = features.shape
    slots = tiles.shape[0]
    wide = width // PARTS
    sibling = (r, c + 1 - 2 * core)
    counter = iter(range(1000))
    local_counter = iter(range(1000))

    def copy(source, target, landing, device):
        slot = next(counter)
        out = pltpu.make_async_remote_copy(source, target, send.at[slot], recv.at[slot], device, MESH)
        into = pltpu.make_async_remote_copy(landing, landing, send.at[slot], recv.at[slot], device, MESH)
        return out, into

    def bring(source, target):
        moved = pltpu.make_async_copy(source, target, local.at[next(local_counter)])
        moved.start()
        return moved

    def columns(p):
        return pl.ds(p * wide, wide)

    barrier = pltpu.get_barrier_semaphore()
    row_peers = [(lax.rem(r + d, n_row), c) for d in range(1, n_row)]
    col_peers = [(r, lax.rem(c + d, n_col)) for d in range(1, n_col)]
    for peer in row_peers + col_peers:
        pl.semaphore_signal(barrier, inc=1, device_id=peer, device_id_type=MESH)
    own_feats = [bring(features.at[:, columns(p)], slabs[p].at[r]) for p in range(PARTS)]
    tiles_here = bring(tiles_in, tiles)
    weight_here = bring(weight_in, weight)
    cotangent_here = bring(cotangent_in, cotangent)
    pl.semaphore_wait(barrier, len(row_peers) + len(col_peers))

    sent = []

    def start(out):
        out.start()
        sent.append(out)

    gathers = []
    for p in range(PARTS):
        gathers.append([])
        for d in range(1, n_row):
            out, into = copy(features.at[:, columns(p)], slabs[p].at[r],
                             slabs[p].at[lax.rem(r + n_row - d, n_row)], (lax.rem(r + d, n_row), c))
            start(out)
            gathers[p].append(into)

    live = count[0, 0]
    offsets = [lax.rem(rows[0, s] - c + n_col, n_col) for s in range(slots)]
    tiles_here.wait()
    for k in range(REACH):
        for s in range(slots):
            masked[k, :, s * size:(s + 1) * size] = jnp.where(
                jnp.logical_and(offsets[s] == k, s < live), tiles[s], jnp.zeros_like(tiles[s])
            )
    for moved in own_feats:
        moved.wait()
    weight_here.wait()
    feats = jnp.concatenate([slabs[p][r] for p in range(PARTS)], axis=1)
    self_part[...] = dot(feats, weight[:width])
    cotangent_here.wait()

    sums = []
    for p in range(PARTS):
        for into in gathers[p]:
            into.wait_recv()
        for s in range(slots):
            chosen[p, s * size:(s + 1) * size, :] = slabs[p][cols[0, s]]
        part[p, 0] = dot(masked[1 + 2 * core], chosen[p]).astype(jnp.bfloat16)
        out, straight = copy(part.at[p, 0], arrived.at[p, 0], arrived.at[p, 0],
                             (r, lax.rem(c + 1 + 2 * core, n_col)))
        start(out)
        swap[p] = dot(masked[3 - 2 * core], chosen[p])
        out, into = copy(swap.at[p], swap_in.at[p], swap_in.at[p], sibling)
        start(out)
        joined = dot(masked[2], chosen[p])
        own_part[p] = dot(masked[0], chosen[p])
        into.wait_recv()
        part[p, 1] = (joined + swap_in[p]).astype(jnp.bfloat16)
        out, into = copy(part.at[p, 1], arrived.at[p, 1], arrived.at[p, 1], (r, lax.rem(c + 2, n_col)))
        start(out)
        sums.append([straight, into])

    first = core == 0
    lefts = []
    highs, lows = [], []
    for p in range(PARTS):
        total = own_part[p]
        for k, into in enumerate(sums[p]):
            into.wait_recv()
            total = total + arrived[p, k].astype(jnp.float32)
        high, low = split(total)
        highs.append(high)
        lows.append(low)
        mine = slabs[p][r]
        empty = jnp.zeros_like(high)
        give[p, 0] = jnp.where(first, high, mine)
        give[p, 1] = jnp.where(first, low, empty)
        out, into = copy(give.at[p], taken.at[p], taken.at[p], sibling)
        start(out)
        lefts.append(into)
        left_high[p * wide:(p + 1) * wide, :size] = jnp.where(first, mine, high).T
        left_low[p * wide:(p + 1) * wide, :size] = jnp.where(first, empty, low).T

    high = jnp.concatenate(highs, axis=1)
    low = jnp.concatenate(lows, axis=1)
    ups = []
    for p in range(PARTS):
        at = slice(p * wide, (p + 1) * wide)
        pre_act = self_part[:, at] + dot(high, weight[width:, at]) + dot(low, weight[width:, at])
        gate = 1.0 / (1.0 + jnp.exp(-pre_act))
        slope = gate * (1.0 + pre_act * (1.0 - gate))
        up_give[p] = (cotangent[:, at].astype(jnp.float32) * slope).astype(jnp.bfloat16)
        out, into = copy(up_give.at[p], up_taken.at[p], up_taken.at[p], sibling)
        start(out)
        ups.append(into)
        hidden[:, at] = (pre_act * gate).astype(jnp.bfloat16)
    for p in range(PARTS):
        lefts[p].wait_recv()
        left_high[p * wide:(p + 1) * wide, size:] = taken[p, 0].T
        left_low[p * wide:(p + 1) * wide, size:] = taken[p, 1].T

    share = width // n_row
    small = share // n_z

    def block(half, q, level, p):
        return grad.at[pl.ds(pl.multiple_of(half * width + q * share + level * small, small), small), columns(p)]

    def band(half, q, p):
        return grad.at[pl.ds(pl.multiple_of(half * width + q * share, share), share), columns(p)]

    waiting = []
    for p in range(PARTS):
        ups[p].wait_recv()
        upstream = jnp.concatenate([up_give[p], up_taken[p]], axis=0)
        waiting.append([])
        for d in range(n_row - 1, -1, -1):
            q = lax.rem(r + d, n_row)
            at = pl.ds(pl.multiple_of(q * share, share), share)
            value = dot(left_high[at, :], upstream) + dot(left_low[at, :], upstream)
            if d == 0:
                piece[p] = value
                continue
            term[p, d - 1] = value.astype(jnp.bfloat16)
            out, into = copy(term.at[p, d - 1], term_in.at[p, d - 1], term_in.at[p, d - 1], (q, c))
            start(out)
            waiting[p].append((d, into))
    over_z = []
    for p in range(PARTS):
        total = piece[p]
        for d, into in waiting[p]:
            into.wait_recv()
            total = total + term_in[p, d - 1].astype(jnp.float32)
        piece[p] = total
        over_z.append([])
        for d in range(n_z - 1, 0, -1):
            q = flip(z, d)
            at = pl.ds(pl.multiple_of(q * small, small), small)
            if d == 1:
                out, into = copy(piece.at[p, at], near_in.at[p], near_in.at[p], (r, 2 * q + core))
            else:
                far[p, d - 2] = piece[p, at, :].astype(jnp.bfloat16)
                out, into = copy(far.at[p, d - 2], far_in.at[p, d - 2], far_in.at[p, d - 2], (r, 2 * q + core))
            start(out)
            over_z[p].append((d, into))

    back_z = []
    for p in range(PARTS):
        total = piece[p, pl.ds(pl.multiple_of(z * small, small), small), :]
        for d, into in over_z[p]:
            into.wait_recv()
            total = total + (near_in[p] if d == 1 else far_in[p, d - 2].astype(jnp.float32))
        mine = block(core, r, z, p)
        mine[...] = (total * scale).astype(jnp.bfloat16)
        back_z.append([])
        for d in range(1, n_z):
            out, into = copy(mine, mine, block(core, r, lax.rem(z + n_z - d, n_z), p),
                             (r, 2 * lax.rem(z + d, n_z) + core))
            start(out)
            back_z[p].append(into)
    back_row = []
    last = []

    placed = []

    def deliver(half, q, p):
        at = (pl.ds(pl.multiple_of(half * width + q * share, share), share), columns(p))
        wide_grad[at] = grad[at].astype(jnp.float32)
        placed.append(bring(wide_grad.at[at], grad_out.at[at]))

    def pass_on(q, p):
        out, into = copy(band(core, q, p), band(core, q, p), band(1 - core, q, p), sibling)
        start(out)
        last.append((into, q, p))
        deliver(core, q, p)

    for p in range(PARTS):
        for into in back_z[p]:
            into.wait_recv()
        mine = band(core, r, p)
        back_row.append([])
        for d in range(1, n_row):
            q = lax.rem(r + n_row - d, n_row)
            out, into = copy(mine, mine, band(core, q, p), (lax.rem(r + d, n_row), c))
            start(out)
            back_row[p].append((q, into))
        pass_on(r, p)
    for p in range(PARTS):
        for q, into in back_row[p]:
            into.wait_recv()
            pass_on(q, p)
    for into, q, p in last:
        into.wait_recv()
        deliver(1 - core, q, p)
    for moved in placed:
        moved.wait()
    for out in sent:
        out.wait_send()


def fused(features, tiles, rows, cols, count, weight, cotangent, n_row, n_col):
    size, width = features.shape
    slots = tiles.shape[0]
    wide = width // PARTS
    share = width // n_row
    n_z = n_col // 2
    small = share // n_z
    half, full = jnp.bfloat16, jnp.float32
    copies = PARTS * (3 * (n_row - 1) + (REACH - 1) + 2 * (n_z - 1) + 2 + n_row)
    hbm = pl.BlockSpec(memory_space=pl.ANY)
    vmem = pl.BlockSpec(memory_space=pltpu.VMEM)
    smem = pl.BlockSpec(memory_space=pltpu.SMEM)
    return pl.pallas_call(
        functools.partial(kernel, n_row, n_col, float(size * n_row * n_col) ** (-0.5)),
        out_shape=(
            jax.ShapeDtypeStruct((size, width), half),
            jax.ShapeDtypeStruct((2 * width, width), full),
        ),
        in_specs=[hbm, hbm, smem, smem, smem, hbm, hbm],
        out_specs=(vmem, hbm),
        scratch_shapes=[
            pltpu.VMEM(tiles.shape, half),
            pltpu.VMEM(weight.shape, half),
            pltpu.VMEM((size, width), half),
            pltpu.VMEM((2 * width, width), half),
            pltpu.VMEM((2 * width, width), full),
            pltpu.VMEM((REACH, size, slots * size), half),
            pltpu.VMEM((PARTS, slots * size, wide), half),
            pltpu.VMEM((PARTS, 2, size, wide), half),
            pltpu.VMEM((PARTS, 2, size, wide), half),
            pltpu.VMEM((PARTS, size, wide), full),
            pltpu.VMEM((PARTS, size, wide), full),
            pltpu.VMEM((width, 2 * size), half),
            pltpu.VMEM((width, 2 * size), half),
            pltpu.VMEM((PARTS, 2, size, wide), half),
            pltpu.VMEM((PARTS, 2, size, wide), half),
            pltpu.VMEM((PARTS, size, wide), half),
            pltpu.VMEM((PARTS, size, wide), half),
            pltpu.VMEM((PARTS, n_row - 1, share, wide), half),
            pltpu.VMEM((PARTS, n_row - 1, share, wide), half),
            pltpu.VMEM((PARTS, share, wide), full),
            pltpu.VMEM((PARTS, small, wide), full),
            pltpu.VMEM((PARTS, n_z - 2, small, wide), half),
            pltpu.VMEM((PARTS, n_z - 2, small, wide), half),
            pltpu.VMEM((PARTS, size, wide), full),
            pltpu.VMEM((size, width), full),
            pltpu.SemaphoreType.DMA((copies,)),
            pltpu.SemaphoreType.DMA((copies,)),
            pltpu.SemaphoreType.DMA((PARTS + 3 + 2 * PARTS * n_row,)),
            *[pltpu.VMEM((n_row, size, wide), half)] * PARTS,
        ],
        compiler_params=pltpu.CompilerParams(
            collective_id=0, has_side_effects=True, vmem_limit_bytes=60 * 1024 * 1024
        ),
    )(features, tiles, rows, cols, count, weight, cotangent)


def body(features, adj_tiles, tile_rows, tile_cols, tile_count, weight, cotangent):
    width = features.shape[1]
    own_nodes = features.shape[0]
    row_count = lax.axis_size("row")
    col_count = lax.axis_size("col")
    tiles = adj_tiles[0]
    slots, size = tiles.shape[:2]
    share = width // row_count
    flippable = col_count // 2 in (4, 8, 16, 32)
    small = share // (col_count // 2)
    if REACH == 4 and col_count % 2 == 0 and flippable and small >= 16 and small % 16 == 0:
        hidden, grad = fused(
            features, tiles, tile_rows, tile_cols, tile_count, weight, cotangent, row_count, col_count
        )
        return hidden, grad
    position = lax.axis_index("col")
    offsets = (tile_rows[0] - position) % col_count
    live = jnp.arange(slots) < tile_count[0, 0]
    col_feats = lax.all_gather(features, "row", axis=0, tiled=True)
    chosen = jnp.take(col_feats.reshape(-1, size, width), tile_cols[0], axis=0).reshape(slots * size, width)
    placed = (offsets[None, :] == jnp.arange(REACH)[:, None]) & live[None, :]
    masked = jnp.where(placed[:, None, :, None], tiles.transpose(1, 0, 2)[None], 0)
    sums = dot(masked.reshape(REACH * size, slots * size), chosen).reshape(REACH, size, width)
    total = sums[0]
    for step in range(1, REACH):
        total = total + from_behind(sums[step], "col", step)
    high, low = split(total)
    pre_act = dot(features, weight[:width]) + dot(high, weight[width:]) + dot(low, weight[width:])
    hidden = jax.nn.silu(pre_act).astype(jnp.bfloat16)
    sigmoid_z = jax.nn.sigmoid(pre_act)
    slope = sigmoid_z * (1.0 + pre_act * (1.0 - sigmoid_z))
    upstream = (cotangent.astype(jnp.float32) * slope).astype(jnp.bfloat16)
    grad_self = dot(features.T, upstream)
    grad_neigh = dot(high.T, upstream) + dot(low.T, upstream)
    stacked = jnp.concatenate([grad_self, grad_neigh], axis=0)
    summed = lax.psum(stacked, ("row", "col"))
    total_nodes = own_nodes * row_count * col_count
    return hidden, summed * float(total_nodes) ** (-0.5)


def solution(mesh):
    in_specs = (
        P(("row", "col"), None),
        P("row", "col", None, None),
        P("row", "col"),
        P("row", "col"),
        P("row", "col"),
        P(),
        P(("row", "col"), None),
    )
    out_specs = (P(("row", "col"), None), P())
    return jax.shard_map(body, mesh=mesh, in_specs=in_specs, out_specs=out_specs, check_vma=False)
```

```python
import functools

import jax
import jax.numpy as jnp
from jax import lax
from jax.experimental import pallas as pl
from jax.experimental.pallas import tpu as pltpu
from jax.sharding import PartitionSpec as P

REACH = 4


def from_behind(value, axis, steps):
    count = lax.axis_size(axis)
    pairs = [(source, (source + steps) % count) for source in range(count)]
    return lax.ppermute(value, axis, pairs)


def split(value):
    high = value.astype(jnp.bfloat16)
    return high, (value - high.astype(jnp.float32)).astype(jnp.bfloat16)


def dot(a, b):
    return jnp.dot(a, b, preferred_element_type=jnp.float32)


MESH = pl.DeviceIdType.MESH
PARTS = 2


def flip(index, bits):
    for bit in (1, 2, 4, 8, 16):
        if bits & bit:
            index = index + bit - 2 * bit * lax.rem(lax.div(index, bit), 2)
    return index


def kernel(n_row, n_col, scale, features, tiles_in, rows, cols, count, weight_in, cotangent_in, hidden, grad,
           tiles, weight, cotangent, masked, chosen, part, arrived, swap, swap_in, left_high, left_low,
           give, taken, up_give, up_taken, term, term_in, piece, near_in, far, far_in, own_part, self_part, send, recv, local, *slabs):
    r, c = lax.axis_index("row"), lax.axis_index("col")
    core, z = lax.rem(c, 2), lax.div(c, 2)
    n_z = n_col // 2
    size, width = features.shape
    slots = tiles.shape[0]
    wide = width // PARTS
    sibling = (r, c + 1 - 2 * core)
    counter = iter(range(1000))
    local_counter = iter(range(1000))

    def copy(source, target, landing, device):
        slot = next(counter)
        out = pltpu.make_async_remote_copy(source, target, send.at[slot], recv.at[slot], device, MESH)
        into = pltpu.make_async_remote_copy(landing, landing, send.at[slot], recv.at[slot], device, MESH)
        return out, into

    def bring(source, target):
        moved = pltpu.make_async_copy(source, target, local.at[next(local_counter)])
        moved.start()
        return moved

    def columns(p):
        return pl.ds(p * wide, wide)

    barrier = pltpu.get_barrier_semaphore()
    row_peers = [(lax.rem(r + d, n_row), c) for d in range(1, n_row)]
    col_peers = [(r, lax.rem(c + d, n_col)) for d in range(1, n_col)]
    for peer in row_peers + col_peers:
        pl.semaphore_signal(barrier, inc=1, device_id=peer, device_id_type=MESH)
    own_feats = [bring(features.at[:, columns(p)], slabs[p].at[r]) for p in range(PARTS)]
    tiles_here = bring(tiles_in, tiles)
    weight_here = bring(weight_in, weight)
    cotangent_here = bring(cotangent_in, cotangent)
    pl.semaphore_wait(barrier, len(row_peers) + len(col_peers))

    sent = []

    def start(out):
        out.start()
        sent.append(out)

    gathers = []
    for p in range(PARTS):
        gathers.append([])
        for d in range(1, n_row):
            out, into = copy(features.at[:, columns(p)], slabs[p].at[r],
                             slabs[p].at[lax.rem(r + n_row - d, n_row)], (lax.rem(r + d, n_row), c))
            start(out)
            gathers[p].append(into)

    live = count[0, 0]
    offsets = [lax.rem(rows[0, s] - c + n_col, n_col) for s in range(slots)]
    tiles_here.wait()
    for k in range(REACH):
        for s in range(slots):
            masked[k, :, s * size:(s + 1) * size] = jnp.where(
                jnp.logical_and(offsets[s] == k, s < live), tiles[s], jnp.zeros_like(tiles[s])
            )
    for moved in own_feats:
        moved.wait()
    weight_here.wait()
    feats = jnp.concatenate([slabs[p][r] for p in range(PARTS)], axis=1)
    self_part[...] = dot(feats, weight[:width])
    cotangent_here.wait()

    sums = []
    for p in range(PARTS):
        for into in gathers[p]:
            into.wait_recv()
        for s in range(slots):
            chosen[p, s * size:(s + 1) * size, :] = slabs[p][cols[0, s]]
        part[p, 0] = dot(masked[1 + 2 * core], chosen[p]).astype(jnp.bfloat16)
        out, straight = copy(part.at[p, 0], arrived.at[p, 0], arrived.at[p, 0],
                             (r, lax.rem(c + 1 + 2 * core, n_col)))
        start(out)
        swap[p] = dot(masked[3 - 2 * core], chosen[p])
        out, into = copy(swap.at[p], swap_in.at[p], swap_in.at[p], sibling)
        start(out)
        joined = dot(masked[2], chosen[p])
        own_part[p] = dot(masked[0], chosen[p])
        into.wait_recv()
        part[p, 1] = (joined + swap_in[p]).astype(jnp.bfloat16)
        out, into = copy(part.at[p, 1], arrived.at[p, 1], arrived.at[p, 1], (r, lax.rem(c + 2, n_col)))
        start(out)
        sums.append([straight, into])

    first = core == 0
    lefts = []
    highs, lows = [], []
    for p in range(PARTS):
        total = own_part[p]
        for k, into in enumerate(sums[p]):
            into.wait_recv()
            total = total + arrived[p, k].astype(jnp.float32)
        high, low = split(total)
        highs.append(high)
        lows.append(low)
        mine = slabs[p][r]
        empty = jnp.zeros_like(high)
        give[p, 0] = jnp.where(first, high, mine)
        give[p, 1] = jnp.where(first, low, empty)
        out, into = copy(give.at[p], taken.at[p], taken.at[p], sibling)
        start(out)
        lefts.append(into)
        left_high[p * wide:(p + 1) * wide, :size] = jnp.where(first, mine, high).T
        left_low[p * wide:(p + 1) * wide, :size] = jnp.where(first, empty, low).T

    high = jnp.concatenate(highs, axis=1)
    low = jnp.concatenate(lows, axis=1)
    ups = []
    for p in range(PARTS):
        at = slice(p * wide, (p + 1) * wide)
        pre_act = self_part[:, at] + dot(high, weight[width:, at]) + dot(low, weight[width:, at])
        gate = 1.0 / (1.0 + jnp.exp(-pre_act))
        slope = gate * (1.0 + pre_act * (1.0 - gate))
        up_give[p] = (cotangent[:, at].astype(jnp.float32) * slope).astype(jnp.bfloat16)
        out, into = copy(up_give.at[p], up_taken.at[p], up_taken.at[p], sibling)
        start(out)
        ups.append(into)
        hidden[:, at] = (pre_act * gate).astype(jnp.bfloat16)
    for p in range(PARTS):
        lefts[p].wait_recv()
        left_high[p * wide:(p + 1) * wide, size:] = taken[p, 0].T
        left_low[p * wide:(p + 1) * wide, size:] = taken[p, 1].T

    share = width // n_row
    small = share // n_z

    def block(half, q, level, p):
        return grad.at[pl.ds(pl.multiple_of(half * width + q * share + level * small, small), small), columns(p)]

    def band(half, q, p):
        return grad.at[pl.ds(pl.multiple_of(half * width + q * share, share), share), columns(p)]

    waiting = []
    for p in range(PARTS):
        ups[p].wait_recv()
        upstream = jnp.concatenate([up_give[p], up_taken[p]], axis=0)
        waiting.append([])
        for d in range(n_row - 1, -1, -1):
            q = lax.rem(r + d, n_row)
            at = pl.ds(pl.multiple_of(q * share, share), share)
            value = dot(left_high[at, :], upstream) + dot(left_low[at, :], upstream)
            if d == 0:
                piece[p] = value
                continue
            term[p, d - 1] = value.astype(jnp.bfloat16)
            out, into = copy(term.at[p, d - 1], term_in.at[p, d - 1], term_in.at[p, d - 1], (q, c))
            start(out)
            waiting[p].append((d, into))
    over_z = []
    for p in range(PARTS):
        total = piece[p]
        for d, into in waiting[p]:
            into.wait_recv()
            total = total + term_in[p, d - 1].astype(jnp.float32)
        piece[p] = total
        over_z.append([])
        for d in range(n_z - 1, 0, -1):
            q = flip(z, d)
            at = pl.ds(pl.multiple_of(q * small, small), small)
            if d == 1:
                out, into = copy(piece.at[p, at], near_in.at[p], near_in.at[p], (r, 2 * q + core))
            else:
                far[p, d - 2] = piece[p, at, :].astype(jnp.bfloat16)
                out, into = copy(far.at[p, d - 2], far_in.at[p, d - 2], far_in.at[p, d - 2], (r, 2 * q + core))
            start(out)
            over_z[p].append((d, into))

    back_z = []
    for p in range(PARTS):
        total = piece[p, pl.ds(pl.multiple_of(z * small, small), small), :]
        for d, into in over_z[p]:
            into.wait_recv()
            total = total + (near_in[p] if d == 1 else far_in[p, d - 2].astype(jnp.float32))
        mine = block(core, r, z, p)
        mine[...] = (total * scale).astype(jnp.bfloat16)
        back_z.append([])
        for d in range(1, n_z):
            out, into = copy(mine, mine, block(core, r, lax.rem(z + n_z - d, n_z), p),
                             (r, 2 * lax.rem(z + d, n_z) + core))
            start(out)
            back_z[p].append(into)
    back_row = []
    last = []

    def pass_on(q, p):
        out, into = copy(band(core, q, p), band(core, q, p), band(1 - core, q, p), sibling)
        start(out)
        last.append((into, q, p))

    for p in range(PARTS):
        for into in back_z[p]:
            into.wait_recv()
        mine = band(core, r, p)
        back_row.append([])
        for d in range(1, n_row):
            q = lax.rem(r + n_row - d, n_row)
            out, into = copy(mine, mine, band(core, q, p), (lax.rem(r + d, n_row), c))
            start(out)
            back_row[p].append((q, into))
        pass_on(r, p)
    for p in range(PARTS):
        for q, into in back_row[p]:
            into.wait_recv()
            pass_on(q, p)
    for into, q, p in last:
        into.wait_recv()
    for out in sent:
        out.wait_send()


def fused(features, tiles, rows, cols, count, weight, cotangent, n_row, n_col):
    size, width = features.shape
    slots = tiles.shape[0]
    wide = width // PARTS
    share = width // n_row
    n_z = n_col // 2
    small = share // n_z
    half, full = jnp.bfloat16, jnp.float32
    copies = PARTS * (3 * (n_row - 1) + (REACH - 1) + 2 * (n_z - 1) + 2 + n_row)
    hbm = pl.BlockSpec(memory_space=pl.ANY)
    vmem = pl.BlockSpec(memory_space=pltpu.VMEM)
    smem = pl.BlockSpec(memory_space=pltpu.SMEM)
    return pl.pallas_call(
        functools.partial(kernel, n_row, n_col, float(size * n_row * n_col) ** (-0.5)),
        out_shape=(
            pltpu.VMEM((size, width), half),
            pltpu.VMEM((2 * width, width), half),
        ),
        in_specs=[hbm, hbm, smem, smem, smem, hbm, hbm],
        out_specs=(vmem, vmem),
        scratch_shapes=[
            pltpu.VMEM(tiles.shape, half),
            pltpu.VMEM(weight.shape, half),
            pltpu.VMEM((size, width), half),
            pltpu.VMEM((REACH, size, slots * size), half),
            pltpu.VMEM((PARTS, slots * size, wide), half),
            pltpu.VMEM((PARTS, 2, size, wide), half),
            pltpu.VMEM((PARTS, 2, size, wide), half),
            pltpu.VMEM((PARTS, size, wide), full),
            pltpu.VMEM((PARTS, size, wide), full),
            pltpu.VMEM((width, 2 * size), half),
            pltpu.VMEM((width, 2 * size), half),
            pltpu.VMEM((PARTS, 2, size, wide), half),
            pltpu.VMEM((PARTS, 2, size, wide), half),
            pltpu.VMEM((PARTS, size, wide), half),
            pltpu.VMEM((PARTS, size, wide), half),
            pltpu.VMEM((PARTS, n_row - 1, share, wide), half),
            pltpu.VMEM((PARTS, n_row - 1, share, wide), half),
            pltpu.VMEM((PARTS, share, wide), full),
            pltpu.VMEM((PARTS, small, wide), full),
            pltpu.VMEM((PARTS, n_z - 2, small, wide), half),
            pltpu.VMEM((PARTS, n_z - 2, small, wide), half),
            pltpu.VMEM((PARTS, size, wide), full),
            pltpu.VMEM((size, width), full),
            pltpu.SemaphoreType.DMA((copies,)),
            pltpu.SemaphoreType.DMA((copies,)),
            pltpu.SemaphoreType.DMA((PARTS + 3,)),
            *[pltpu.VMEM((n_row, size, wide), half)] * PARTS,
        ],
        compiler_params=pltpu.CompilerParams(
            collective_id=0, has_side_effects=True, vmem_limit_bytes=60 * 1024 * 1024
        ),
    )(features, tiles, rows, cols, count, weight, cotangent)


def body(features, adj_tiles, tile_rows, tile_cols, tile_count, weight, cotangent):
    width = features.shape[1]
    own_nodes = features.shape[0]
    row_count = lax.axis_size("row")
    col_count = lax.axis_size("col")
    tiles = adj_tiles[0]
    slots, size = tiles.shape[:2]
    share = width // row_count
    flippable = col_count // 2 in (4, 8, 16, 32)
    small = share // (col_count // 2)
    if REACH == 4 and col_count % 2 == 0 and flippable and small >= 16 and small % 16 == 0:
        hidden, grad = fused(
            features, tiles, tile_rows, tile_cols, tile_count, weight, cotangent, row_count, col_count
        )
        return hidden, grad.astype(jnp.float32)
    position = lax.axis_index("col")
    offsets = (tile_rows[0] - position) % col_count
    live = jnp.arange(slots) < tile_count[0, 0]
    col_feats = lax.all_gather(features, "row", axis=0, tiled=True)
    chosen = jnp.take(col_feats.reshape(-1, size, width), tile_cols[0], axis=0).reshape(slots * size, width)
    placed = (offsets[None, :] == jnp.arange(REACH)[:, None]) & live[None, :]
    masked = jnp.where(placed[:, None, :, None], tiles.transpose(1, 0, 2)[None], 0)
    sums = dot(masked.reshape(REACH * size, slots * size), chosen).reshape(REACH, size, width)
    total = sums[0]
    for step in range(1, REACH):
        total = total + from_behind(sums[step], "col", step)
    high, low = split(total)
    pre_act = dot(features, weight[:width]) + dot(high, weight[width:]) + dot(low, weight[width:])
    hidden = jax.nn.silu(pre_act).astype(jnp.bfloat16)
    sigmoid_z = jax.nn.sigmoid(pre_act)
    slope = sigmoid_z * (1.0 + pre_act * (1.0 - sigmoid_z))
    upstream = (cotangent.astype(jnp.float32) * slope).astype(jnp.bfloat16)
    grad_self = dot(features.T, upstream)
    grad_neigh = dot(high.T, upstream) + dot(low.T, upstream)
    stacked = jnp.concatenate([grad_self, grad_neigh], axis=0)
    summed = lax.psum(stacked, ("row", "col"))
    total_nodes = own_nodes * row_count * col_count
    return hidden, summed * float(total_nodes) ** (-0.5)


def solution(mesh):
    in_specs = (
        P(("row", "col"), None),
        P("row", "col", None, None),
        P("row", "col"),
        P("row", "col"),
        P("row", "col"),
        P(),
        P(("row", "col"), None),
    )
    out_specs = (P(("row", "col"), None), P())
    return jax.shard_map(body, mesh=mesh, in_specs=in_specs, out_specs=out_specs, check_vma=False)
```

```python
import functools

import jax
import jax.numpy as jnp
from jax import lax
from jax.experimental import pallas as pl
from jax.experimental.pallas import tpu as pltpu
from jax.sharding import PartitionSpec as P

REACH = 4


def from_behind(value, axis, steps):
    count = lax.axis_size(axis)
    pairs = [(source, (source + steps) % count) for source in range(count)]
    return lax.ppermute(value, axis, pairs)


def split(value):
    high = value.astype(jnp.bfloat16)
    return high, (value - high.astype(jnp.float32)).astype(jnp.bfloat16)


def dot(a, b):
    return jnp.dot(a, b, preferred_element_type=jnp.float32)


MESH = pl.DeviceIdType.MESH
PARTS = 2


def flip(index, bits):
    for bit in (1, 2, 4, 8, 16):
        if bits & bit:
            index = index + bit - 2 * bit * lax.rem(lax.div(index, bit), 2)
    return index


def kernel(n_row, n_col, scale, features, tiles_in, rows, cols, count, weight_in, cotangent_in, hidden, grad,
           tiles, weight, cotangent, masked, chosen, part, arrived, swap, swap_in, left_high, left_low,
           give, taken, up_give, up_taken, whole, term, term_in, near, near_in, far, far_in, own_part, self_part, send, recv, local, *slabs):
    r, c = lax.axis_index("row"), lax.axis_index("col")
    core, z = lax.rem(c, 2), lax.div(c, 2)
    n_z = n_col // 2
    size, width = features.shape
    slots = tiles.shape[0]
    wide = width // PARTS
    sibling = (r, c + 1 - 2 * core)
    counter = iter(range(1000))
    local_counter = iter(range(1000))

    def copy(source, target, landing, device):
        slot = next(counter)
        out = pltpu.make_async_remote_copy(source, target, send.at[slot], recv.at[slot], device, MESH)
        into = pltpu.make_async_remote_copy(landing, landing, send.at[slot], recv.at[slot], device, MESH)
        return out, into

    def bring(source, target):
        moved = pltpu.make_async_copy(source, target, local.at[next(local_counter)])
        moved.start()
        return moved

    def columns(p):
        return pl.ds(p * wide, wide)

    barrier = pltpu.get_barrier_semaphore()
    row_peers = [(lax.rem(r + d, n_row), c) for d in range(1, n_row)]
    col_peers = [(r, lax.rem(c + d, n_col)) for d in range(1, n_col)]
    for peer in row_peers + col_peers:
        pl.semaphore_signal(barrier, inc=1, device_id=peer, device_id_type=MESH)
    own_feats = [bring(features.at[:, columns(p)], slabs[p].at[r]) for p in range(PARTS)]
    tiles_here = bring(tiles_in, tiles)
    weight_here = bring(weight_in, weight)
    cotangent_here = bring(cotangent_in, cotangent)
    pl.semaphore_wait(barrier, len(row_peers) + len(col_peers))

    sent = []

    def start(out):
        out.start()
        sent.append(out)

    gathers = []
    for p in range(PARTS):
        gathers.append([])
        for d in range(1, n_row):
            out, into = copy(features.at[:, columns(p)], slabs[p].at[r],
                             slabs[p].at[lax.rem(r + n_row - d, n_row)], (lax.rem(r + d, n_row), c))
            start(out)
            gathers[p].append(into)

    live = count[0, 0]
    offsets = [lax.rem(rows[0, s] - c + n_col, n_col) for s in range(slots)]
    tiles_here.wait()
    for k in range(REACH):
        for s in range(slots):
            masked[k, :, s * size:(s + 1) * size] = jnp.where(
                jnp.logical_and(offsets[s] == k, s < live), tiles[s], jnp.zeros_like(tiles[s])
            )
    for moved in own_feats:
        moved.wait()
    weight_here.wait()
    feats = jnp.concatenate([slabs[p][r] for p in range(PARTS)], axis=1)
    self_part[...] = dot(feats, weight[:width])
    cotangent_here.wait()

    sums = []
    for p in range(PARTS):
        for into in gathers[p]:
            into.wait_recv()
        for s in range(slots):
            chosen[p, s * size:(s + 1) * size, :] = slabs[p][cols[0, s]]
        part[p, 0] = dot(masked[1 + 2 * core], chosen[p]).astype(jnp.bfloat16)
        out, straight = copy(part.at[p, 0], arrived.at[p, 0], arrived.at[p, 0],
                             (r, lax.rem(c + 1 + 2 * core, n_col)))
        start(out)
        swap[p] = dot(masked[3 - 2 * core], chosen[p])
        out, into = copy(swap.at[p], swap_in.at[p], swap_in.at[p], sibling)
        start(out)
        joined = dot(masked[2], chosen[p])
        own_part[p] = dot(masked[0], chosen[p])
        into.wait_recv()
        part[p, 1] = (joined + swap_in[p]).astype(jnp.bfloat16)
        out, into = copy(part.at[p, 1], arrived.at[p, 1], arrived.at[p, 1], (r, lax.rem(c + 2, n_col)))
        start(out)
        sums.append([straight, into])

    share = width // n_row
    small = share // n_z
    first = core == 0

    def place(target, p, at, value):
        for j in range(wide // small):
            q, rest = divmod(p * wide + j * small, share)
            target[rest // small, q * small:(q + 1) * small, at] = value[j * small:(j + 1) * small]

    def place_own(p, high, low):
        place(left_high, p, slice(0, size), jnp.where(first, slabs[p][r], high).T)
        place(left_low, p, slice(0, size), jnp.where(first, jnp.zeros_like(low), low).T)

    lefts = []
    for p in range(PARTS):
        total = own_part[p]
        for k, into in enumerate(sums[p]):
            into.wait_recv()
            total = total + arrived[p, k].astype(jnp.float32)
        high, low = split(total)
        give[p, 0] = jnp.where(first, high, slabs[p][r])
        give[p, 1] = jnp.where(first, low, jnp.zeros_like(low))
        out, into = copy(give.at[p], taken.at[p], taken.at[p], sibling)
        start(out)
        lefts.append(into)
        if p < PARTS - 1:
            below = weight[width + p * wide:width + (p + 1) * wide]
            self_part[...] += dot(high, below) + dot(low, below)
            place_own(p, high, low)

    ups = []
    for p in range(PARTS):
        at = slice(p * wide, (p + 1) * wide)
        below = weight[2 * width - wide:, at]
        pre_act = self_part[:, at] + dot(high, below) + dot(low, below)
        gate = 1.0 / (1.0 + jnp.exp(-pre_act))
        slope = gate * (1.0 + pre_act * (1.0 - gate))
        up_give[:, at] = (cotangent[:, at].astype(jnp.float32) * slope).astype(jnp.bfloat16)
        out, into = copy(up_give.at[:, at], up_taken.at[:, at], up_taken.at[:, at], sibling)
        start(out)
        ups.append(into)
        hidden[:, at] = (pre_act * gate).astype(jnp.bfloat16)
    place_own(PARTS - 1, high, low)
    for p in range(PARTS):
        lefts[p].wait_recv()
        place(left_high, p, slice(size, 2 * size), taken[p, 0].T)
        place(left_low, p, slice(size, 2 * size), taken[p, 1].T)
    for into in ups:
        into.wait_recv()
    upstream = jnp.concatenate([up_give[...], up_taken[...]], axis=0)

    over_row = []
    for i in range(n_z):
        level = flip(z, n_z - 1 - i)
        value = dot(left_high[level], upstream) + dot(left_low[level], upstream)
        whole[i] = value
        term[i] = value.astype(jnp.bfloat16)
        over_row.append([])
        for e in range(1, n_row):
            q = lax.rem(r + e, n_row)
            at = pl.ds(pl.multiple_of(q * small, small), small)
            out, into = copy(term.at[i, at], term_in.at[i, e - 1], term_in.at[i, e - 1], (q, c))
            start(out)
            over_row[i].append(into)
    over_z = []
    for i in range(n_z):
        d = n_z - 1 - i
        device = (r, 2 * flip(z, d) + core)
        total = whole[i, pl.ds(pl.multiple_of(r * small, small), small), :]
        for e, into in enumerate(over_row[i]):
            into.wait_recv()
            total = total + term_in[i, e].astype(jnp.float32)
        if d == 0:
            break
        if d == 1:
            near[...] = total
            out, into = copy(near, near_in, near_in, device)
        else:
            far[d - 2] = total.astype(jnp.bfloat16)
            out, into = copy(far.at[d - 2], far_in.at[d - 2], far_in.at[d - 2], device)
        start(out)
        over_z.append((d, into))
    for d, into in over_z:
        into.wait_recv()
        total = total + (near_in[...] if d == 1 else far_in[d - 2].astype(jnp.float32))

    def block(half, q, level):
        return grad.at[pl.ds(pl.multiple_of(half * width + q * share + level * small, small), small)]

    mine = block(core, r, z)
    mine[...] = (total * scale).astype(jnp.bfloat16)
    back_z = []
    for d in range(n_z - 1, 0, -1):
        out, into = copy(mine, mine, block(core, r, flip(z, d)), (r, 2 * flip(z, d) + core))
        start(out)
        back_z.append(into)
    back_z.reverse()
    back_row = []
    last = []

    def pass_on(q, level):
        out, into = copy(block(core, q, level), block(core, q, level), block(1 - core, q, level), sibling)
        start(out)
        last.append(into)

    for d in range(n_z):
        level = flip(z, d)
        if d > 0:
            back_z[d - 1].wait_recv()
        for e in range(1, n_row):
            q = lax.rem(r + n_row - e, n_row)
            out, into = copy(block(core, r, level), block(core, r, level), block(core, q, level),
                             (lax.rem(r + e, n_row), c))
            start(out)
            back_row.append((q, level, into))
        pass_on(r, level)
    for q, level, into in back_row:
        into.wait_recv()
        pass_on(q, level)
    for into in last:
        into.wait_recv()
    for out in sent:
        out.wait_send()


def fused(features, tiles, rows, cols, count, weight, cotangent, n_row, n_col):
    size, width = features.shape
    slots = tiles.shape[0]
    wide = width // PARTS
    share = width // n_row
    n_z = n_col // 2
    small = share // n_z
    half, full = jnp.bfloat16, jnp.float32
    copies = PARTS * (n_row + 4) + 2 * n_z * (n_row - 1) + 2 * (n_z - 1) + n_z * n_row
    hbm = pl.BlockSpec(memory_space=pl.ANY)
    vmem = pl.BlockSpec(memory_space=pltpu.VMEM)
    smem = pl.BlockSpec(memory_space=pltpu.SMEM)
    return pl.pallas_call(
        functools.partial(kernel, n_row, n_col, float(size * n_row * n_col) ** (-0.5)),
        out_shape=(
            pltpu.VMEM((size, width), half),
            pltpu.VMEM((2 * width, width), half),
        ),
        in_specs=[hbm, hbm, smem, smem, smem, hbm, hbm],
        out_specs=(vmem, vmem),
        scratch_shapes=[
            pltpu.VMEM(tiles.shape, half),
            pltpu.VMEM(weight.shape, half),
            pltpu.VMEM((size, width), half),
            pltpu.VMEM((REACH, size, slots * size), half),
            pltpu.VMEM((PARTS, slots * size, wide), half),
            pltpu.VMEM((PARTS, 2, size, wide), half),
            pltpu.VMEM((PARTS, 2, size, wide), half),
            pltpu.VMEM((PARTS, size, wide), full),
            pltpu.VMEM((PARTS, size, wide), full),
            pltpu.VMEM((n_z, n_row * small, 2 * size), half),
            pltpu.VMEM((n_z, n_row * small, 2 * size), half),
            pltpu.VMEM((PARTS, 2, size, wide), half),
            pltpu.VMEM((PARTS, 2, size, wide), half),
            pltpu.VMEM((size, width), half),
            pltpu.VMEM((size, width), half),
            pltpu.VMEM((n_z, n_row * small, width), full),
            pltpu.VMEM((n_z, n_row * small, width), half),
            pltpu.VMEM((n_z, n_row - 1, small, width), half),
            pltpu.VMEM((small, width), full),
            pltpu.VMEM((small, width), full),
            pltpu.VMEM((n_z - 2, small, width), half),
            pltpu.VMEM((n_z - 2, small, width), half),
            pltpu.VMEM((PARTS, size, wide), full),
            pltpu.VMEM((size, width), full),
            pltpu.SemaphoreType.DMA((copies,)),
            pltpu.SemaphoreType.DMA((copies,)),
            pltpu.SemaphoreType.DMA((PARTS + 3,)),
            *[pltpu.VMEM((n_row, size, wide), half)] * PARTS,
        ],
        compiler_params=pltpu.CompilerParams(
            collective_id=0, has_side_effects=True, vmem_limit_bytes=60 * 1024 * 1024
        ),
    )(features, tiles, rows, cols, count, weight, cotangent)


def body(features, adj_tiles, tile_rows, tile_cols, tile_count, weight, cotangent):
    width = features.shape[1]
    own_nodes = features.shape[0]
    row_count = lax.axis_size("row")
    col_count = lax.axis_size("col")
    tiles = adj_tiles[0]
    slots, size = tiles.shape[:2]
    share = width // row_count
    flippable = col_count // 2 in (4, 8, 16, 32)
    small = share // (col_count // 2)
    if REACH == 4 and col_count % 2 == 0 and flippable and small >= 16 and small % 16 == 0:
        hidden, grad = fused(
            features, tiles, tile_rows, tile_cols, tile_count, weight, cotangent, row_count, col_count
        )
        return hidden, grad.astype(jnp.float32)
    position = lax.axis_index("col")
    offsets = (tile_rows[0] - position) % col_count
    live = jnp.arange(slots) < tile_count[0, 0]
    col_feats = lax.all_gather(features, "row", axis=0, tiled=True)
    chosen = jnp.take(col_feats.reshape(-1, size, width), tile_cols[0], axis=0).reshape(slots * size, width)
    placed = (offsets[None, :] == jnp.arange(REACH)[:, None]) & live[None, :]
    masked = jnp.where(placed[:, None, :, None], tiles.transpose(1, 0, 2)[None], 0)
    sums = dot(masked.reshape(REACH * size, slots * size), chosen).reshape(REACH, size, width)
    total = sums[0]
    for step in range(1, REACH):
        total = total + from_behind(sums[step], "col", step)
    high, low = split(total)
    pre_act = dot(features, weight[:width]) + dot(high, weight[width:]) + dot(low, weight[width:])
    hidden = jax.nn.silu(pre_act).astype(jnp.bfloat16)
    sigmoid_z = jax.nn.sigmoid(pre_act)
    slope = sigmoid_z * (1.0 + pre_act * (1.0 - sigmoid_z))
    upstream = (cotangent.astype(jnp.float32) * slope).astype(jnp.bfloat16)
    grad_self = dot(features.T, upstream)
    grad_neigh = dot(high.T, upstream) + dot(low.T, upstream)
    stacked = jnp.concatenate([grad_self, grad_neigh], axis=0)
    summed = lax.psum(stacked, ("row", "col"))
    total_nodes = own_nodes * row_count * col_count
    return hidden, summed * float(total_nodes) ** (-0.5)


def solution(mesh):
    in_specs = (
        P(("row", "col"), None),
        P("row", "col", None, None),
        P("row", "col"),
        P("row", "col"),
        P("row", "col"),
        P(),
        P(("row", "col"), None),
    )
    out_specs = (P(("row", "col"), None), P())
    return jax.shard_map(body, mesh=mesh, in_specs=in_specs, out_specs=out_specs, check_vma=False)
```

```python
import functools

import jax
import jax.numpy as jnp
from jax import lax
from jax.experimental import pallas as pl
from jax.experimental.pallas import tpu as pltpu
from jax.sharding import PartitionSpec as P

REACH = 4


def from_behind(value, axis, steps):
    count = lax.axis_size(axis)
    pairs = [(source, (source + steps) % count) for source in range(count)]
    return lax.ppermute(value, axis, pairs)


def split(value):
    high = value.astype(jnp.bfloat16)
    return high, (value - high.astype(jnp.float32)).astype(jnp.bfloat16)


def dot(a, b):
    return jnp.dot(a, b, preferred_element_type=jnp.float32)


MESH = pl.DeviceIdType.MESH
PARTS = 4


def flip(index, bits):
    for bit in (1, 2, 4, 8, 16):
        if bits & bit:
            index = index + bit - 2 * bit * lax.rem(lax.div(index, bit), 2)
    return index


def kernel(n_row, n_col, scale, features, tiles_in, rows, cols, count, weight_in, cotangent_in, hidden, grad,
           tiles, weight, cotangent, masked, chosen, part, arrived, swap, swap_in, left_high, left_low,
           give, taken, up_give, up_taken, whole, term, term_in, near, near_in, far, far_in, own_part, self_part, send, recv, local, *slabs):
    r, c = lax.axis_index("row"), lax.axis_index("col")
    core, z = lax.rem(c, 2), lax.div(c, 2)
    n_z = n_col // 2
    size, width = features.shape
    slots = tiles.shape[0]
    wide = width // PARTS
    sibling = (r, c + 1 - 2 * core)
    counter = iter(range(1000))
    local_counter = iter(range(1000))

    def copy(source, target, landing, device):
        slot = next(counter)
        out = pltpu.make_async_remote_copy(source, target, send.at[slot], recv.at[slot], device, MESH)
        into = pltpu.make_async_remote_copy(landing, landing, send.at[slot], recv.at[slot], device, MESH)
        return out, into

    def bring(source, target):
        moved = pltpu.make_async_copy(source, target, local.at[next(local_counter)])
        moved.start()
        return moved

    def columns(p):
        return pl.ds(p * wide, wide)

    barrier = pltpu.get_barrier_semaphore()
    row_peers = [(lax.rem(r + d, n_row), c) for d in range(1, n_row)]
    col_peers = [(r, lax.rem(c + d, n_col)) for d in range(1, n_col)]
    for peer in row_peers + col_peers:
        pl.semaphore_signal(barrier, inc=1, device_id=peer, device_id_type=MESH)
    own_feats = [bring(features.at[:, columns(p)], slabs[p].at[r]) for p in range(PARTS)]
    tiles_here = bring(tiles_in, tiles)
    weight_here = bring(weight_in, weight)
    cotangent_here = bring(cotangent_in, cotangent)
    pl.semaphore_wait(barrier, len(row_peers) + len(col_peers))

    sent = []

    def start(out):
        out.start()
        sent.append(out)

    gathers = []
    for p in range(PARTS):
        gathers.append([])
        for d in range(1, n_row):
            out, into = copy(features.at[:, columns(p)], slabs[p].at[r],
                             slabs[p].at[lax.rem(r + n_row - d, n_row)], (lax.rem(r + d, n_row), c))
            start(out)
            gathers[p].append(into)

    live = count[0, 0]
    offsets = [lax.rem(rows[0, s] - c + n_col, n_col) for s in range(slots)]
    tiles_here.wait()
    for k in range(REACH):
        for s in range(slots):
            masked[k, :, s * size:(s + 1) * size] = jnp.where(
                jnp.logical_and(offsets[s] == k, s < live), tiles[s], jnp.zeros_like(tiles[s])
            )
    for moved in own_feats:
        moved.wait()
    weight_here.wait()
    feats = jnp.concatenate([slabs[p][r] for p in range(PARTS)], axis=1)
    self_part[...] = dot(feats, weight[:width])
    cotangent_here.wait()

    sums = []
    for p in range(PARTS):
        for into in gathers[p]:
            into.wait_recv()
        for s in range(slots):
            chosen[p, s * size:(s + 1) * size, :] = slabs[p][cols[0, s]]
        part[p, 0] = dot(masked[1 + 2 * core], chosen[p]).astype(jnp.bfloat16)
        out, straight = copy(part.at[p, 0], arrived.at[p, 0], arrived.at[p, 0],
                             (r, lax.rem(c + 1 + 2 * core, n_col)))
        start(out)
        swap[p] = dot(masked[3 - 2 * core], chosen[p])
        out, into = copy(swap.at[p], swap_in.at[p], swap_in.at[p], sibling)
        start(out)
        joined = dot(masked[2], chosen[p])
        own_part[p] = dot(masked[0], chosen[p])
        into.wait_recv()
        part[p, 1] = (joined + swap_in[p]).astype(jnp.bfloat16)
        out, into = copy(part.at[p, 1], arrived.at[p, 1], arrived.at[p, 1], (r, lax.rem(c + 2, n_col)))
        start(out)
        sums.append([straight, into])

    share = width // n_row
    small = share // n_z
    first = core == 0

    def place(target, p, at, value):
        for j in range(wide // small):
            q, rest = divmod(p * wide + j * small, share)
            target[rest // small, q * small:(q + 1) * small, at] = value[j * small:(j + 1) * small]

    def place_own(p, high, low):
        place(left_high, p, slice(0, size), jnp.where(first, slabs[p][r], high).T)
        place(left_low, p, slice(0, size), jnp.where(first, jnp.zeros_like(low), low).T)

    def place_sibling(p):
        lefts[p].wait_recv()
        place(left_high, p, slice(size, 2 * size), taken[p, 0].T)
        place(left_low, p, slice(size, 2 * size), taken[p, 1].T)

    lefts = []
    for p in range(PARTS):
        total = own_part[p]
        for k, into in enumerate(sums[p]):
            into.wait_recv()
            total = total + arrived[p, k].astype(jnp.float32)
        high, low = split(total)
        give[p, 0] = jnp.where(first, high, slabs[p][r])
        give[p, 1] = jnp.where(first, low, jnp.zeros_like(low))
        out, into = copy(give.at[p], taken.at[p], taken.at[p], sibling)
        start(out)
        lefts.append(into)
        if p < PARTS - 1:
            below = weight[width + p * wide:width + (p + 1) * wide]
            self_part[...] += dot(high, below) + dot(low, below)
            place_own(p, high, low)
            if p > 0:
                place_sibling(p - 1)

    ups = []
    for p in range(PARTS):
        at = slice(p * wide, (p + 1) * wide)
        below = weight[2 * width - wide:, at]
        pre_act = self_part[:, at] + dot(high, below) + dot(low, below)
        gate = 1.0 / (1.0 + jnp.exp(-pre_act))
        slope = gate * (1.0 + pre_act * (1.0 - gate))
        up_give[:, at] = (cotangent[:, at].astype(jnp.float32) * slope).astype(jnp.bfloat16)
        out, into = copy(up_give.at[:, at], up_taken.at[:, at], up_taken.at[:, at], sibling)
        start(out)
        ups.append(into)
        hidden[:, at] = (pre_act * gate).astype(jnp.bfloat16)
    place_own(PARTS - 1, high, low)
    for p in range(PARTS - 2, PARTS):
        place_sibling(p)
    for into in ups:
        into.wait_recv()
    upstream = jnp.concatenate([up_give[...], up_taken[...]], axis=0)

    over_row = []
    for i in range(n_z):
        level = flip(z, n_z - 1 - i)
        value = dot(left_high[level], upstream) + dot(left_low[level], upstream)
        whole[i] = value
        term[i] = value.astype(jnp.bfloat16)
        over_row.append([])
        for e in range(1, n_row):
            q = lax.rem(r + e, n_row)
            at = pl.ds(pl.multiple_of(q * small, small), small)
            out, into = copy(term.at[i, at], term_in.at[i, e - 1], term_in.at[i, e - 1], (q, c))
            start(out)
            over_row[i].append(into)
    over_z = []
    for i in range(n_z):
        d = n_z - 1 - i
        device = (r, 2 * flip(z, d) + core)
        total = whole[i, pl.ds(pl.multiple_of(r * small, small), small), :]
        for e, into in enumerate(over_row[i]):
            into.wait_recv()
            total = total + term_in[i, e].astype(jnp.float32)
        if d == 0:
            break
        if d == 1:
            near[...] = total
            out, into = copy(near, near_in, near_in, device)
        else:
            far[d - 2] = total.astype(jnp.bfloat16)
            out, into = copy(far.at[d - 2], far_in.at[d - 2], far_in.at[d - 2], device)
        start(out)
        over_z.append((d, into))
    for d, into in over_z:
        into.wait_recv()
        total = total + (near_in[...] if d == 1 else far_in[d - 2].astype(jnp.float32))

    def block(half, q, level):
        return grad.at[pl.ds(pl.multiple_of(half * width + q * share + level * small, small), small)]

    mine = block(core, r, z)
    mine[...] = (total * scale).astype(jnp.bfloat16)
    back_z = []
    for d in range(n_z - 1, 0, -1):
        out, into = copy(mine, mine, block(core, r, flip(z, d)), (r, 2 * flip(z, d) + core))
        start(out)
        back_z.append(into)
    back_z.reverse()
    back_row = []
    last = []

    def pass_on(q, level):
        out, into = copy(block(core, q, level), block(core, q, level), block(1 - core, q, level), sibling)
        start(out)
        last.append(into)

    for d in range(n_z):
        level = flip(z, d)
        if d > 0:
            back_z[d - 1].wait_recv()
        for e in range(1, n_row):
            q = lax.rem(r + n_row - e, n_row)
            out, into = copy(block(core, r, level), block(core, r, level), block(core, q, level),
                             (lax.rem(r + e, n_row), c))
            start(out)
            back_row.append((q, level, into))
        pass_on(r, level)
    for q, level, into in back_row:
        into.wait_recv()
        pass_on(q, level)
    for into in last:
        into.wait_recv()
    for out in sent:
        out.wait_send()


def fused(features, tiles, rows, cols, count, weight, cotangent, n_row, n_col):
    size, width = features.shape
    slots = tiles.shape[0]
    wide = width // PARTS
    share = width // n_row
    n_z = n_col // 2
    small = share // n_z
    half, full = jnp.bfloat16, jnp.float32
    copies = PARTS * (n_row + 4) + 2 * n_z * (n_row - 1) + 2 * (n_z - 1) + n_z * n_row
    hbm = pl.BlockSpec(memory_space=pl.ANY)
    vmem = pl.BlockSpec(memory_space=pltpu.VMEM)
    smem = pl.BlockSpec(memory_space=pltpu.SMEM)
    return pl.pallas_call(
        functools.partial(kernel, n_row, n_col, float(size * n_row * n_col) ** (-0.5)),
        out_shape=(
            pltpu.VMEM((size, width), half),
            pltpu.VMEM((2 * width, width), half),
        ),
        in_specs=[hbm, hbm, smem, smem, smem, hbm, hbm],
        out_specs=(vmem, vmem),
        scratch_shapes=[
            pltpu.VMEM(tiles.shape, half),
            pltpu.VMEM(weight.shape, half),
            pltpu.VMEM((size, width), half),
            pltpu.VMEM((REACH, size, slots * size), half),
            pltpu.VMEM((PARTS, slots * size, wide), half),
            pltpu.VMEM((PARTS, 2, size, wide), half),
            pltpu.VMEM((PARTS, 2, size, wide), half),
            pltpu.VMEM((PARTS, size, wide), full),
            pltpu.VMEM((PARTS, size, wide), full),
            pltpu.VMEM((n_z, n_row * small, 2 * size), half),
            pltpu.VMEM((n_z, n_row * small, 2 * size), half),
            pltpu.VMEM((PARTS, 2, size, wide), half),
            pltpu.VMEM((PARTS, 2, size, wide), half),
            pltpu.VMEM((size, width), half),
            pltpu.VMEM((size, width), half),
            pltpu.VMEM((n_z, n_row * small, width), full),
            pltpu.VMEM((n_z, n_row * small, width), half),
            pltpu.VMEM((n_z, n_row - 1, small, width), half),
            pltpu.VMEM((small, width), full),
            pltpu.VMEM((small, width), full),
            pltpu.VMEM((n_z - 2, small, width), half),
            pltpu.VMEM((n_z - 2, small, width), half),
            pltpu.VMEM((PARTS, size, wide), full),
            pltpu.VMEM((size, width), full),
            pltpu.SemaphoreType.DMA((copies,)),
            pltpu.SemaphoreType.DMA((copies,)),
            pltpu.SemaphoreType.DMA((PARTS + 3,)),
            *[pltpu.VMEM((n_row, size, wide), half)] * PARTS,
        ],
        compiler_params=pltpu.CompilerParams(
            collective_id=0, has_side_effects=True, vmem_limit_bytes=60 * 1024 * 1024
        ),
    )(features, tiles, rows, cols, count, weight, cotangent)


def body(features, adj_tiles, tile_rows, tile_cols, tile_count, weight, cotangent):
    width = features.shape[1]
    own_nodes = features.shape[0]
    row_count = lax.axis_size("row")
    col_count = lax.axis_size("col")
    tiles = adj_tiles[0]
    slots, size = tiles.shape[:2]
    share = width // row_count
    flippable = col_count // 2 in (4, 8, 16, 32)
    small = share // (col_count // 2)
    if REACH == 4 and col_count % 2 == 0 and flippable and small >= 16 and small % 16 == 0:
        hidden, grad = fused(
            features, tiles, tile_rows, tile_cols, tile_count, weight, cotangent, row_count, col_count
        )
        return hidden, grad.astype(jnp.float32)
    position = lax.axis_index("col")
    offsets = (tile_rows[0] - position) % col_count
    live = jnp.arange(slots) < tile_count[0, 0]
    col_feats = lax.all_gather(features, "row", axis=0, tiled=True)
    chosen = jnp.take(col_feats.reshape(-1, size, width), tile_cols[0], axis=0).reshape(slots * size, width)
    placed = (offsets[None, :] == jnp.arange(REACH)[:, None]) & live[None, :]
    masked = jnp.where(placed[:, None, :, None], tiles.transpose(1, 0, 2)[None], 0)
    sums = dot(masked.reshape(REACH * size, slots * size), chosen).reshape(REACH, size, width)
    total = sums[0]
    for step in range(1, REACH):
        total = total + from_behind(sums[step], "col", step)
    high, low = split(total)
    pre_act = dot(features, weight[:width]) + dot(high, weight[width:]) + dot(low, weight[width:])
    hidden = jax.nn.silu(pre_act).astype(jnp.bfloat16)
    sigmoid_z = jax.nn.sigmoid(pre_act)
    slope = sigmoid_z * (1.0 + pre_act * (1.0 - sigmoid_z))
    upstream = (cotangent.astype(jnp.float32) * slope).astype(jnp.bfloat16)
    grad_self = dot(features.T, upstream)
    grad_neigh = dot(high.T, upstream) + dot(low.T, upstream)
    stacked = jnp.concatenate([grad_self, grad_neigh], axis=0)
    summed = lax.psum(stacked, ("row", "col"))
    total_nodes = own_nodes * row_count * col_count
    return hidden, summed * float(total_nodes) ** (-0.5)


def solution(mesh):
    in_specs = (
        P(("row", "col"), None),
        P("row", "col", None, None),
        P("row", "col"),
        P("row", "col"),
        P("row", "col"),
        P(),
        P(("row", "col"), None),
    )
    out_specs = (P(("row", "col"), None), P())
    return jax.shard_map(body, mesh=mesh, in_specs=in_specs, out_specs=out_specs, check_vma=False)
```

```python
import functools

import jax
import jax.numpy as jnp
from jax import lax
from jax.experimental import pallas as pl
from jax.experimental.pallas import tpu as pltpu
from jax.sharding import PartitionSpec as P

REACH = 4


def from_behind(value, axis, steps):
    count = lax.axis_size(axis)
    pairs = [(source, (source + steps) % count) for source in range(count)]
    return lax.ppermute(value, axis, pairs)


def split(value):
    high = value.astype(jnp.bfloat16)
    return high, (value - high.astype(jnp.float32)).astype(jnp.bfloat16)


def dot(a, b):
    return jnp.dot(a, b, preferred_element_type=jnp.float32)


MESH = pl.DeviceIdType.MESH
PARTS = 2


def flip(index, bits):
    for bit in (1, 2, 4, 8, 16):
        if bits & bit:
            index = index + bit - 2 * bit * lax.rem(lax.div(index, bit), 2)
    return index


def kernel(n_row, n_col, scale, features, tiles_in, rows, cols, count, weight_in, cotangent_in, hidden, grad,
           tiles, weight, cotangent, masked, chosen, part, arrived, swap, swap_in, left_high, left_low,
           give, taken, up_give, up_taken, whole, term, term_in, near, near_in, far, far_in, own_part, self_part, send, recv, local, *slabs):
    r, c = lax.axis_index("row"), lax.axis_index("col")
    core, z = lax.rem(c, 2), lax.div(c, 2)
    n_z = n_col // 2
    size, width = features.shape
    slots = tiles.shape[0]
    wide = width // PARTS
    sibling = (r, c + 1 - 2 * core)
    counter = iter(range(1000))
    local_counter = iter(range(1000))

    def copy(source, target, landing, device):
        slot = next(counter)
        out = pltpu.make_async_remote_copy(source, target, send.at[slot], recv.at[slot], device, MESH)
        into = pltpu.make_async_remote_copy(landing, landing, send.at[slot], recv.at[slot], device, MESH)
        return out, into

    def bring(source, target):
        moved = pltpu.make_async_copy(source, target, local.at[next(local_counter)])
        moved.start()
        return moved

    def columns(p):
        return pl.ds(p * wide, wide)

    barrier = pltpu.get_barrier_semaphore()
    row_peers = [(lax.rem(r + d, n_row), c) for d in range(1, n_row)]
    col_peers = [(r, lax.rem(c + d, n_col)) for d in range(1, n_col)]
    for peer in row_peers + col_peers:
        pl.semaphore_signal(barrier, inc=1, device_id=peer, device_id_type=MESH)
    own_feats = [bring(features.at[:, columns(p)], slabs[p].at[r]) for p in range(PARTS)]
    tiles_here = bring(tiles_in, tiles)
    weight_here = bring(weight_in, weight)
    cotangent_here = bring(cotangent_in, cotangent)
    pl.semaphore_wait(barrier, len(row_peers) + len(col_peers))

    sent = []

    def start(out):
        out.start()
        sent.append(out)

    gathers = []
    for p in range(PARTS):
        gathers.append([])
        for d in range(1, n_row):
            out, into = copy(features.at[:, columns(p)], slabs[p].at[r],
                             slabs[p].at[flip(r, n_row - d)], (flip(r, n_row - d), c))
            start(out)
            gathers[p].append(into)

    live = count[0, 0]
    offsets = [lax.rem(rows[0, s] - c + n_col, n_col) for s in range(slots)]
    tiles_here.wait()
    for k in range(REACH):
        for s in range(slots):
            masked[k, :, s * size:(s + 1) * size] = jnp.where(
                jnp.logical_and(offsets[s] == k, s < live), tiles[s], jnp.zeros_like(tiles[s])
            )
    for moved in own_feats:
        moved.wait()
    weight_here.wait()
    feats = jnp.concatenate([slabs[p][r] for p in range(PARTS)], axis=1)
    self_part[...] = dot(feats, weight[:width])
    cotangent_here.wait()

    sums = []
    for p in range(PARTS):
        for into in gathers[p]:
            into.wait_recv()
        for s in range(slots):
            chosen[p, s * size:(s + 1) * size, :] = slabs[p][cols[0, s]]
        part[p, 0] = dot(masked[1 + 2 * core], chosen[p]).astype(jnp.bfloat16)
        out, straight = copy(part.at[p, 0], arrived.at[p, 0], arrived.at[p, 0],
                             (r, lax.rem(c + 1 + 2 * core, n_col)))
        start(out)
        swap[p] = dot(masked[3 - 2 * core], chosen[p])
        out, into = copy(swap.at[p], swap_in.at[p], swap_in.at[p], sibling)
        start(out)
        joined = dot(masked[2], chosen[p])
        own_part[p] = dot(masked[0], chosen[p])
        into.wait_recv()
        part[p, 1] = (joined + swap_in[p]).astype(jnp.bfloat16)
        out, into = copy(part.at[p, 1], arrived.at[p, 1], arrived.at[p, 1], (r, lax.rem(c + 2, n_col)))
        start(out)
        sums.append([straight, into])

    share = width // n_row
    small = share // n_z
    first = core == 0

    def place(target, p, at, value):
        for j in range(wide // small):
            q, rest = divmod(p * wide + j * small, share)
            target[rest // small, q * small:(q + 1) * small, at] = value[j * small:(j + 1) * small]

    def place_own(p, high, low):
        place(left_high, p, slice(0, size), jnp.where(first, slabs[p][r], high).T)
        place(left_low, p, slice(0, size), jnp.where(first, jnp.zeros_like(low), low).T)

    def place_sibling(p):
        lefts[p].wait_recv()
        place(left_high, p, slice(size, 2 * size), taken[p, 0].T)
        place(left_low, p, slice(size, 2 * size), taken[p, 1].T)

    lefts = []
    for p in range(PARTS):
        if p > 0:
            place_sibling(p - 1)
        total = own_part[p]
        for k, into in enumerate(sums[p]):
            into.wait_recv()
            total = total + arrived[p, k].astype(jnp.float32)
        high, low = split(total)
        give[p, 0] = jnp.where(first, high, slabs[p][r])
        give[p, 1] = jnp.where(first, low, jnp.zeros_like(low))
        out, into = copy(give.at[p], taken.at[p], taken.at[p], sibling)
        start(out)
        lefts.append(into)
        if p < PARTS - 1:
            below = weight[width + p * wide:width + (p + 1) * wide]
            self_part[...] += dot(high, below) + dot(low, below)
            place_own(p, high, low)

    ups = []
    for p in range(PARTS):
        at = slice(p * wide, (p + 1) * wide)
        below = weight[2 * width - wide:, at]
        pre_act = self_part[:, at] + dot(high, below) + dot(low, below)
        gate = 1.0 / (1.0 + jnp.exp(-pre_act))
        slope = gate * (1.0 + pre_act * (1.0 - gate))
        up_give[:, at] = (cotangent[:, at].astype(jnp.float32) * slope).astype(jnp.bfloat16)
        out, into = copy(up_give.at[:, at], up_taken.at[:, at], up_taken.at[:, at], sibling)
        start(out)
        ups.append(into)
        hidden[:, at] = (pre_act * gate).astype(jnp.bfloat16)
    place_own(PARTS - 1, high, low)
    place_sibling(PARTS - 1)
    for into in ups:
        into.wait_recv()
    upstream = jnp.concatenate([up_give[...], up_taken[...]], axis=0)

    over_row = []
    for i in range(n_z):
        level = flip(z, n_z - 1 - i)
        value = dot(left_high[level], upstream) + dot(left_low[level], upstream)
        whole[i] = value
        term[i] = value.astype(jnp.bfloat16)
        over_row.append([])
        for e in range(1, n_row):
            q = flip(r, n_row - e)
            at = pl.ds(pl.multiple_of(q * small, small), small)
            out, into = copy(term.at[i, at], term_in.at[i, e - 1], term_in.at[i, e - 1], (q, c))
            start(out)
            over_row[i].append(into)
    over_z = []
    for i in range(n_z):
        d = n_z - 1 - i
        device = (r, 2 * flip(z, d) + core)
        total = whole[i, pl.ds(pl.multiple_of(r * small, small), small), :]
        for e, into in enumerate(over_row[i]):
            into.wait_recv()
            total = total + term_in[i, e].astype(jnp.float32)
        if d == 0:
            break
        if d == 1:
            near[...] = total
            out, into = copy(near, near_in, near_in, device)
        else:
            far[d - 2] = total.astype(jnp.bfloat16)
            out, into = copy(far.at[d - 2], far_in.at[d - 2], far_in.at[d - 2], device)
        start(out)
        over_z.append((d, into))
    for d, into in over_z:
        into.wait_recv()
        total = total + (near_in[...] if d == 1 else far_in[d - 2].astype(jnp.float32))

    def block(half, q, level):
        return grad.at[pl.ds(pl.multiple_of(half * width + q * share + level * small, small), small)]

    mine = block(core, r, z)
    mine[...] = (total * scale).astype(jnp.bfloat16)
    back_z = []
    for d in range(n_z - 1, 0, -1):
        out, into = copy(mine, mine, block(core, r, flip(z, d)), (r, 2 * flip(z, d) + core))
        start(out)
        back_z.append(into)
    back_z.reverse()
    back_row = []
    last = []

    def pass_on(q, level):
        out, into = copy(block(core, q, level), block(core, q, level), block(1 - core, q, level), sibling)
        start(out)
        last.append(into)

    for d in range(n_z):
        level = flip(z, d)
        if d > 0:
            back_z[d - 1].wait_recv()
        for e in range(1, n_row):
            q = flip(r, n_row - e)
            out, into = copy(block(core, r, level), block(core, r, level), block(core, q, level),
                             (q, c))
            start(out)
            back_row.append((q, level, into))
        pass_on(r, level)
    for q, level, into in back_row:
        into.wait_recv()
        pass_on(q, level)
    for into in last:
        into.wait_recv()
    for out in sent:
        out.wait_send()


def fused(features, tiles, rows, cols, count, weight, cotangent, n_row, n_col):
    size, width = features.shape
    slots = tiles.shape[0]
    wide = width // PARTS
    share = width // n_row
    n_z = n_col // 2
    small = share // n_z
    half, full = jnp.bfloat16, jnp.float32
    copies = PARTS * (n_row + 4) + 2 * n_z * (n_row - 1) + 2 * (n_z - 1) + n_z * n_row
    hbm = pl.BlockSpec(memory_space=pl.ANY)
    vmem = pl.BlockSpec(memory_space=pltpu.VMEM)
    smem = pl.BlockSpec(memory_space=pltpu.SMEM)
    return pl.pallas_call(
        functools.partial(kernel, n_row, n_col, float(size * n_row * n_col) ** (-0.5)),
        out_shape=(
            pltpu.VMEM((size, width), half),
            pltpu.VMEM((2 * width, width), half),
        ),
        in_specs=[hbm, hbm, smem, smem, smem, hbm, hbm],
        out_specs=(vmem, vmem),
        scratch_shapes=[
            pltpu.VMEM(tiles.shape, half),
            pltpu.VMEM(weight.shape, half),
            pltpu.VMEM((size, width), half),
            pltpu.VMEM((REACH, size, slots * size), half),
            pltpu.VMEM((PARTS, slots * size, wide), half),
            pltpu.VMEM((PARTS, 2, size, wide), half),
            pltpu.VMEM((PARTS, 2, size, wide), half),
            pltpu.VMEM((PARTS, size, wide), full),
            pltpu.VMEM((PARTS, size, wide), full),
            pltpu.VMEM((n_z, n_row * small, 2 * size), half),
            pltpu.VMEM((n_z, n_row * small, 2 * size), half),
            pltpu.VMEM((PARTS, 2, size, wide), half),
            pltpu.VMEM((PARTS, 2, size, wide), half),
            pltpu.VMEM((size, width), half),
            pltpu.VMEM((size, width), half),
            pltpu.VMEM((n_z, n_row * small, width), full),
            pltpu.VMEM((n_z, n_row * small, width), half),
            pltpu.VMEM((n_z, n_row - 1, small, width), half),
            pltpu.VMEM((small, width), full),
            pltpu.VMEM((small, width), full),
            pltpu.VMEM((n_z - 2, small, width), half),
            pltpu.VMEM((n_z - 2, small, width), half),
            pltpu.VMEM((PARTS, size, wide), full),
            pltpu.VMEM((size, width), full),
            pltpu.SemaphoreType.DMA((copies,)),
            pltpu.SemaphoreType.DMA((copies,)),
            pltpu.SemaphoreType.DMA((PARTS + 3,)),
            *[pltpu.VMEM((n_row, size, wide), half)] * PARTS,
        ],
        compiler_params=pltpu.CompilerParams(
            collective_id=0, has_side_effects=True, vmem_limit_bytes=60 * 1024 * 1024
        ),
    )(features, tiles, rows, cols, count, weight, cotangent)


def body(features, adj_tiles, tile_rows, tile_cols, tile_count, weight, cotangent):
    width = features.shape[1]
    own_nodes = features.shape[0]
    row_count = lax.axis_size("row")
    col_count = lax.axis_size("col")
    tiles = adj_tiles[0]
    slots, size = tiles.shape[:2]
    share = width // row_count
    flippable = col_count // 2 in (4, 8, 16, 32) and row_count in (2, 4, 8, 16)
    small = share // (col_count // 2)
    if REACH == 4 and col_count % 2 == 0 and flippable and small >= 16 and small % 16 == 0:
        hidden, grad = fused(
            features, tiles, tile_rows, tile_cols, tile_count, weight, cotangent, row_count, col_count
        )
        return hidden, grad.astype(jnp.float32)
    position = lax.axis_index("col")
    offsets = (tile_rows[0] - position) % col_count
    live = jnp.arange(slots) < tile_count[0, 0]
    col_feats = lax.all_gather(features, "row", axis=0, tiled=True)
    chosen = jnp.take(col_feats.reshape(-1, size, width), tile_cols[0], axis=0).reshape(slots * size, width)
    placed = (offsets[None, :] == jnp.arange(REACH)[:, None]) & live[None, :]
    masked = jnp.where(placed[:, None, :, None], tiles.transpose(1, 0, 2)[None], 0)
    sums = dot(masked.reshape(REACH * size, slots * size), chosen).reshape(REACH, size, width)
    total = sums[0]
    for step in range(1, REACH):
        total = total + from_behind(sums[step], "col", step)
    high, low = split(total)
    pre_act = dot(features, weight[:width]) + dot(high, weight[width:]) + dot(low, weight[width:])
    hidden = jax.nn.silu(pre_act).astype(jnp.bfloat16)
    sigmoid_z = jax.nn.sigmoid(pre_act)
    slope = sigmoid_z * (1.0 + pre_act * (1.0 - sigmoid_z))
    upstream = (cotangent.astype(jnp.float32) * slope).astype(jnp.bfloat16)
    grad_self = dot(features.T, upstream)
    grad_neigh = dot(high.T, upstream) + dot(low.T, upstream)
    stacked = jnp.concatenate([grad_self, grad_neigh], axis=0)
    summed = lax.psum(stacked, ("row", "col"))
    total_nodes = own_nodes * row_count * col_count
    return hidden, summed * float(total_nodes) ** (-0.5)


def solution(mesh):
    in_specs = (
        P(("row", "col"), None),
        P("row", "col", None, None),
        P("row", "col"),
        P("row", "col"),
        P("row", "col"),
        P(),
        P(("row", "col"), None),
    )
    out_specs = (P(("row", "col"), None), P())
    return jax.shard_map(body, mesh=mesh, in_specs=in_specs, out_specs=out_specs, check_vma=False)
```

```python
import functools

import jax
import jax.numpy as jnp
from jax import lax
from jax.experimental import pallas as pl
from jax.experimental.pallas import tpu as pltpu
from jax.sharding import PartitionSpec as P

REACH = 4


def from_behind(value, axis, steps):
    count = lax.axis_size(axis)
    pairs = [(source, (source + steps) % count) for source in range(count)]
    return lax.ppermute(value, axis, pairs)


def split(value):
    high = value.astype(jnp.bfloat16)
    return high, (value - high.astype(jnp.float32)).astype(jnp.bfloat16)


def dot(a, b):
    return jnp.dot(a, b, preferred_element_type=jnp.float32)


MESH = pl.DeviceIdType.MESH
PARTS = 2


def flip(index, bits):
    for bit in (1, 2, 4, 8, 16):
        if bits & bit:
            index = index + bit - 2 * bit * lax.rem(lax.div(index, bit), 2)
    return index


def kernel(n_row, n_col, scale, features, tiles_in, rows, cols, count, weight_in, cotangent_in, hidden, grad,
           tiles, weight, cotangent, masked, chosen, part, arrived, swap, swap_in, left_high, left_low,
           give, taken, up_give, up_taken, whole, term, term_in, near, near_in, far, far_in, own_part, self_part, send, recv, local, *slabs):
    r, c = lax.axis_index("row"), lax.axis_index("col")
    core, z = lax.rem(c, 2), lax.div(c, 2)
    n_z = n_col // 2
    size, width = features.shape
    slots = tiles.shape[0]
    wide = width // PARTS
    sibling = (r, c + 1 - 2 * core)
    counter = iter(range(1000))
    local_counter = iter(range(1000))

    def copy(source, target, landing, device):
        slot = next(counter)
        out = pltpu.make_async_remote_copy(source, target, send.at[slot], recv.at[slot], device, MESH)
        into = pltpu.make_async_remote_copy(landing, landing, send.at[slot], recv.at[slot], device, MESH)
        return out, into

    def bring(source, target):
        moved = pltpu.make_async_copy(source, target, local.at[next(local_counter)])
        moved.start()
        return moved

    def columns(p):
        return pl.ds(p * wide, wide)

    barrier = pltpu.get_barrier_semaphore()
    row_peers = [(lax.rem(r + d, n_row), c) for d in range(1, n_row)]
    col_peers = [(r, lax.rem(c + d, n_col)) for d in range(1, n_col)]
    for peer in row_peers + col_peers:
        pl.semaphore_signal(barrier, inc=1, device_id=peer, device_id_type=MESH)
    own_feats = [bring(features.at[:, columns(p)], slabs[p].at[r]) for p in range(PARTS)]
    tiles_here = bring(tiles_in, tiles)
    weight_here = bring(weight_in, weight)
    cotangent_here = bring(cotangent_in, cotangent)
    pl.semaphore_wait(barrier, len(row_peers) + len(col_peers))

    sent = []

    def start(out):
        out.start()
        sent.append(out)

    gathers = []
    for p in range(PARTS):
        gathers.append([])
        for d in range(1, n_row):
            out, into = copy(features.at[:, columns(p)], slabs[p].at[r],
                             slabs[p].at[flip(r, n_row - d)], (flip(r, n_row - d), c))
            start(out)
            gathers[p].append(into)

    live = count[0, 0]
    offsets = [lax.rem(rows[0, s] - c + n_col, n_col) for s in range(slots)]
    tiles_here.wait()
    for k in range(REACH):
        for s in range(slots):
            masked[k, :, s * size:(s + 1) * size] = jnp.where(
                jnp.logical_and(offsets[s] == k, s < live), tiles[s], jnp.zeros_like(tiles[s])
            )
    for moved in own_feats:
        moved.wait()
    weight_here.wait()
    feats = jnp.concatenate([slabs[p][r] for p in range(PARTS)], axis=1)
    self_part[...] = dot(feats, weight[:width])
    cotangent_here.wait()

    sums = []
    for p in range(PARTS):
        for into in gathers[p]:
            into.wait_recv()
        for s in range(slots):
            chosen[p, s * size:(s + 1) * size, :] = slabs[p][cols[0, s]]
        swap[p] = dot(masked[3 - 2 * core], chosen[p])
        out, joining = copy(swap.at[p], swap_in.at[p], swap_in.at[p], sibling)
        start(out)
        part[p, 0] = dot(masked[1 + 2 * core], chosen[p]).astype(jnp.bfloat16)
        out, straight = copy(part.at[p, 0], arrived.at[p, 0], arrived.at[p, 0],
                             (r, lax.rem(c + 1 + 2 * core, n_col)))
        start(out)
        joined = dot(masked[2], chosen[p])
        own_part[p] = dot(masked[0], chosen[p])
        joining.wait_recv()
        part[p, 1] = (joined + swap_in[p]).astype(jnp.bfloat16)
        out, into = copy(part.at[p, 1], arrived.at[p, 1], arrived.at[p, 1], (r, lax.rem(c + 2, n_col)))
        start(out)
        sums.append([straight, into])

    share = width // n_row
    small = share // n_z
    first = core == 0

    def place(target, p, at, value):
        for j in range(wide // small):
            q, rest = divmod(p * wide + j * small, share)
            target[rest // small, q * small:(q + 1) * small, at] = value[j * small:(j + 1) * small]

    def place_own(p, high, low):
        place(left_high, p, slice(0, size), jnp.where(first, slabs[p][r], high).T)
        place(left_low, p, slice(0, size), jnp.where(first, jnp.zeros_like(low), low).T)

    def place_sibling(p):
        lefts[p].wait_recv()
        place(left_high, p, slice(size, 2 * size), taken[p, 0].T)
        place(left_low, p, slice(size, 2 * size), taken[p, 1].T)

    lefts = []
    for p in range(PARTS):
        if p > 0:
            place_sibling(p - 1)
        total = own_part[p]
        for k, into in enumerate(sums[p]):
            into.wait_recv()
            total = total + arrived[p, k].astype(jnp.float32)
        high, low = split(total)
        give[p, 0] = jnp.where(first, high, slabs[p][r])
        give[p, 1] = jnp.where(first, low, jnp.zeros_like(low))
        out, into = copy(give.at[p], taken.at[p], taken.at[p], sibling)
        start(out)
        lefts.append(into)
        if p < PARTS - 1:
            below = weight[width + p * wide:width + (p + 1) * wide]
            self_part[...] += dot(high, below) + dot(low, below)
            place_own(p, high, low)

    ups = []
    for p in range(PARTS):
        at = slice(p * wide, (p + 1) * wide)
        below = weight[2 * width - wide:, at]
        pre_act = self_part[:, at] + dot(high, below) + dot(low, below)
        gate = 1.0 / (1.0 + jnp.exp(-pre_act))
        slope = gate * (1.0 + pre_act * (1.0 - gate))
        up_give[:, at] = (cotangent[:, at].astype(jnp.float32) * slope).astype(jnp.bfloat16)
        out, into = copy(up_give.at[:, at], up_taken.at[:, at], up_taken.at[:, at], sibling)
        start(out)
        ups.append(into)
        hidden[:, at] = (pre_act * gate).astype(jnp.bfloat16)
    place_own(PARTS - 1, high, low)
    place_sibling(PARTS - 1)
    for into in ups:
        into.wait_recv()
    upstream = jnp.concatenate([up_give[...], up_taken[...]], axis=0)

    over_row = []
    for i in range(n_z):
        level = flip(z, n_z - 1 - i)
        value = dot(left_high[level], upstream) + dot(left_low[level], upstream)
        whole[i] = value
        term[i] = value.astype(jnp.bfloat16)
        over_row.append([])
        for e in range(1, n_row):
            q = flip(r, n_row - e)
            at = pl.ds(pl.multiple_of(q * small, small), small)
            out, into = copy(term.at[i, at], term_in.at[i, e - 1], term_in.at[i, e - 1], (q, c))
            start(out)
            over_row[i].append(into)
    over_z = []
    for i in range(n_z):
        d = n_z - 1 - i
        device = (r, 2 * flip(z, d) + core)
        total = whole[i, pl.ds(pl.multiple_of(r * small, small), small), :]
        for e, into in enumerate(over_row[i]):
            into.wait_recv()
            total = total + term_in[i, e].astype(jnp.float32)
        if d == 0:
            break
        if d == 1:
            near[...] = total
            out, into = copy(near, near_in, near_in, device)
        else:
            far[d - 2] = total.astype(jnp.bfloat16)
            out, into = copy(far.at[d - 2], far_in.at[d - 2], far_in.at[d - 2], device)
        start(out)
        over_z.append((d, into))
    for d, into in over_z:
        into.wait_recv()
        total = total + (near_in[...] if d == 1 else far_in[d - 2].astype(jnp.float32))

    def block(half, q, level):
        return grad.at[pl.ds(pl.multiple_of(half * width + q * share + level * small, small), small)]

    mine = block(core, r, z)
    mine[...] = (total * scale).astype(jnp.bfloat16)
    back_z = []
    for d in range(n_z - 1, 0, -1):
        out, into = copy(mine, mine, block(core, r, flip(z, d)), (r, 2 * flip(z, d) + core))
        start(out)
        back_z.append(into)
    back_z.reverse()
    back_row = []
    last = []

    def pass_on(q, level):
        out, into = copy(block(core, q, level), block(core, q, level), block(1 - core, q, level), sibling)
        start(out)
        last.append(into)

    for d in range(n_z):
        level = flip(z, d)
        if d > 0:
            back_z[d - 1].wait_recv()
        for e in range(1, n_row):
            q = flip(r, n_row - e)
            out, into = copy(block(core, r, level), block(core, r, level), block(core, q, level),
                             (q, c))
            start(out)
            back_row.append((q, level, into))
        pass_on(r, level)
    for q, level, into in back_row:
        into.wait_recv()
        pass_on(q, level)
    for into in last:
        into.wait_recv()
    for out in sent:
        out.wait_send()


def fused(features, tiles, rows, cols, count, weight, cotangent, n_row, n_col):
    size, width = features.shape
    slots = tiles.shape[0]
    wide = width // PARTS
    share = width // n_row
    n_z = n_col // 2
    small = share // n_z
    half, full = jnp.bfloat16, jnp.float32
    copies = PARTS * (n_row + 4) + 2 * n_z * (n_row - 1) + 2 * (n_z - 1) + n_z * n_row
    hbm = pl.BlockSpec(memory_space=pl.ANY)
    vmem = pl.BlockSpec(memory_space=pltpu.VMEM)
    smem = pl.BlockSpec(memory_space=pltpu.SMEM)
    return pl.pallas_call(
        functools.partial(kernel, n_row, n_col, float(size * n_row * n_col) ** (-0.5)),
        out_shape=(
            pltpu.VMEM((size, width), half),
            pltpu.VMEM((2 * width, width), half),
        ),
        in_specs=[hbm, hbm, smem, smem, smem, hbm, hbm],
        out_specs=(vmem, vmem),
        scratch_shapes=[
            pltpu.VMEM(tiles.shape, half),
            pltpu.VMEM(weight.shape, half),
            pltpu.VMEM((size, width), half),
            pltpu.VMEM((REACH, size, slots * size), half),
            pltpu.VMEM((PARTS, slots * size, wide), half),
            pltpu.VMEM((PARTS, 2, size, wide), half),
            pltpu.VMEM((PARTS, 2, size, wide), half),
            pltpu.VMEM((PARTS, size, wide), full),
            pltpu.VMEM((PARTS, size, wide), full),
            pltpu.VMEM((n_z, n_row * small, 2 * size), half),
            pltpu.VMEM((n_z, n_row * small, 2 * size), half),
            pltpu.VMEM((PARTS, 2, size, wide), half),
            pltpu.VMEM((PARTS, 2, size, wide), half),
            pltpu.VMEM((size, width), half),
            pltpu.VMEM((size, width), half),
            pltpu.VMEM((n_z, n_row * small, width), full),
            pltpu.VMEM((n_z, n_row * small, width), half),
            pltpu.VMEM((n_z, n_row - 1, small, width), half),
            pltpu.VMEM((small, width), full),
            pltpu.VMEM((small, width), full),
            pltpu.VMEM((n_z - 2, small, width), half),
            pltpu.VMEM((n_z - 2, small, width), half),
            pltpu.VMEM((PARTS, size, wide), full),
            pltpu.VMEM((size, width), full),
            pltpu.SemaphoreType.DMA((copies,)),
            pltpu.SemaphoreType.DMA((copies,)),
            pltpu.SemaphoreType.DMA((PARTS + 3,)),
            *[pltpu.VMEM((n_row, size, wide), half)] * PARTS,
        ],
        compiler_params=pltpu.CompilerParams(
            collective_id=0, has_side_effects=True, vmem_limit_bytes=60 * 1024 * 1024
        ),
    )(features, tiles, rows, cols, count, weight, cotangent)


CHUNKS = 8


def write_out(hidden, grad, hidden_out, grad_out, wide_grad, sems):
    moves = [pltpu.make_async_copy(hidden, hidden_out, sems.at[CHUNKS])]
    moves[0].start()
    rows = grad.shape[0] // CHUNKS
    for i in range(CHUNKS):
        at = pl.ds(i * rows, rows)
        wide_grad[at] = grad[at].astype(jnp.float32)
        moves.append(pltpu.make_async_copy(wide_grad.at[at], grad_out.at[at], sems.at[i]))
        moves[-1].start()
    for moved in moves:
        moved.wait()


def written(hidden, grad):
    vmem = pl.BlockSpec(memory_space=pltpu.VMEM)
    hbm = pl.BlockSpec(memory_space=pl.ANY)
    return pl.pallas_call(
        write_out,
        out_shape=(
            jax.ShapeDtypeStruct(hidden.shape, hidden.dtype),
            jax.ShapeDtypeStruct(grad.shape, jnp.float32),
        ),
        in_specs=[vmem, vmem],
        out_specs=(hbm, hbm),
        scratch_shapes=[pltpu.VMEM(grad.shape, jnp.float32), pltpu.SemaphoreType.DMA((CHUNKS + 1,))],
        compiler_params=pltpu.CompilerParams(vmem_limit_bytes=40 * 1024 * 1024),
    )(hidden, grad)


def body(features, adj_tiles, tile_rows, tile_cols, tile_count, weight, cotangent):
    width = features.shape[1]
    own_nodes = features.shape[0]
    row_count = lax.axis_size("row")
    col_count = lax.axis_size("col")
    tiles = adj_tiles[0]
    slots, size = tiles.shape[:2]
    share = width // row_count
    flippable = col_count // 2 in (4, 8, 16, 32) and row_count in (2, 4, 8, 16)
    small = share // (col_count // 2)
    if REACH == 4 and col_count % 2 == 0 and flippable and small >= 16 and small % 16 == 0:
        hidden, grad = fused(
            features, tiles, tile_rows, tile_cols, tile_count, weight, cotangent, row_count, col_count
        )
        return written(hidden, grad)
    position = lax.axis_index("col")
    offsets = (tile_rows[0] - position) % col_count
    live = jnp.arange(slots) < tile_count[0, 0]
    col_feats = lax.all_gather(features, "row", axis=0, tiled=True)
    chosen = jnp.take(col_feats.reshape(-1, size, width), tile_cols[0], axis=0).reshape(slots * size, width)
    placed = (offsets[None, :] == jnp.arange(REACH)[:, None]) & live[None, :]
    masked = jnp.where(placed[:, None, :, None], tiles.transpose(1, 0, 2)[None], 0)
    sums = dot(masked.reshape(REACH * size, slots * size), chosen).reshape(REACH, size, width)
    total = sums[0]
    for step in range(1, REACH):
        total = total + from_behind(sums[step], "col", step)
    high, low = split(total)
    pre_act = dot(features, weight[:width]) + dot(high, weight[width:]) + dot(low, weight[width:])
    hidden = jax.nn.silu(pre_act).astype(jnp.bfloat16)
    sigmoid_z = jax.nn.sigmoid(pre_act)
    slope = sigmoid_z * (1.0 + pre_act * (1.0 - sigmoid_z))
    upstream = (cotangent.astype(jnp.float32) * slope).astype(jnp.bfloat16)
    grad_self = dot(features.T, upstream)
    grad_neigh = dot(high.T, upstream) + dot(low.T, upstream)
    stacked = jnp.concatenate([grad_self, grad_neigh], axis=0)
    summed = lax.psum(stacked, ("row", "col"))
    total_nodes = own_nodes * row_count * col_count
    return hidden, summed * float(total_nodes) ** (-0.5)


def solution(mesh):
    in_specs = (
        P(("row", "col"), None),
        P("row", "col", None, None),
        P("row", "col"),
        P("row", "col"),
        P("row", "col"),
        P(),
        P(("row", "col"), None),
    )
    out_specs = (P(("row", "col"), None), P())
    return jax.shard_map(body, mesh=mesh, in_specs=in_specs, out_specs=out_specs, check_vma=False)
```
